512 devices in a mesh: gx: 8 (over z_hi, x), gy: 16 (over y, core), ma: 4 (over z_lo).
Axes of the slice: x: 4, y: 8, z: 8 (z_hi: 2, z_lo: 4; z = z_hi * 4 + z_lo), core: 2. Of those that a mesh axis runs over, the one named last changes fastest.
Arguments:
- pod_modes: bfloat16 [256, 4, 16, 128, 128], P('ma', None, 'gx', 'gy'), may hold values from -6 to 6
- velocity: float32 [3, 16, 128, 128], P(None, 'gx', 'gy'), may hold values from -1 to 1
- region: int32 [16, 128, 128], P('gx', 'gy'), may hold values from 0 to 7
- partner: int32 [128], replicated, may hold values from 0 to 127, each once
- coupling_table: float32 [8, 4, 4], replicated, may hold values from -3 to 3
Outputs:
- reduced: float32 [4, 256, 256], P(None, None, 'ma')
The draws below stay inside these ranges and needn't reach their ends.
Inputs may be any that keep to these rules, and one draw needn't show every extreme that they name: `partner`: each of the 128 plane numbers appears once.
All inputs are finite; a program needn't handle non-finite values.
Results may differ from the reference program's by a relative error of at most 0.0029.
Values may be sent and summed in bfloat16 or wider, within the bound.
No kernel may reach another device: no remote copies, remote signals or barrier semaphores. Data moves between devices by JAX's collectives and lax.ppermute only.
A program may use at most 64 MiB of HBM per device.

```python
import math
import jax
import jax.numpy as jnp
from jax import lax

MODES = 256
FIELDS = 4
REGIONS = 8
NZ = 128
NX = 16
NY = 128


def set_ends(drawn, rng, smallest, high):
    index_at = [jax.random.randint(jax.random.fold_in(rng, axis), (), 0, length) for axis, length in enumerate(drawn.shape)]
    main_axis = drawn.shape.index(max(drawn.shape))
    beside = index_at[:main_axis] + [(index_at[main_axis] + 1) % drawn.shape[main_axis]] + index_at[main_axis + 1:]
    return drawn.at[tuple(index_at)].set(smallest).at[tuple(beside)].set(high)


def steps_of(key, shape, cuts, least, high):
    def one(position, shards_of):
        steps = jax.random.uniform(jax.random.fold_in(jax.random.fold_in(key, 6), position), (shards_of,), jnp.float32, least / len(cuts), high / len(cuts))
        return jnp.repeat(jnp.exp(steps), shape[position] // shards_of).reshape((-1,) + (1,) * (len(shape) - position - 1))

    level = one(*cuts[0])
    for cut in cuts[1:]:
        level = level * one(*cut)
    return level


def gaussian(own_key, dims, spread, bound, pieces=(), kind=jnp.bfloat16):
    loudness = steps_of(own_key, dims, pieces, -0.22, 0.18) if pieces else 1.0
    result = jax.random.normal(own_key, dims, jnp.float32) * spread * loudness
    return jnp.minimum(jnp.maximum(result, -bound), bound).astype(kind)


def setup_inputs(seed: int = 0) -> dict:
    arg_keys = jax.random.split(jax.random.key(seed), 6)
    return {
        "pod_modes": gaussian(arg_keys[0], (MODES, FIELDS, NX, NY, NZ), 1.0, 6.0, ((0, 4), (2, 8), (3, 16))),
        "velocity": jnp.clip(jax.random.uniform(arg_keys[1], (3, NX, NY, NZ), jnp.float32, -1.0, 1.0) * steps_of(arg_keys[1], (3, NX, NY, NZ), ((1, 8), (2, 16)), -0.4, 0.0), -1.0, 1.0),
        "region": set_ends(jax.random.randint(arg_keys[2], (NX, NY, NZ), 0, REGIONS), jax.random.fold_in(arg_keys[2], 1), 0, REGIONS - 1).astype(jnp.int32),
        "partner": jax.random.permutation(arg_keys[3], NZ).astype(jnp.int32),
        "coupling_table": gaussian(arg_keys[4], (REGIONS, FIELDS, FIELDS), 0.5, 3.0, (), jnp.float32),
    }


def coupling_terms(centre, coefficients):
    outputs = []
    for field_out in range(centre.shape[1]):
        running = coefficients[field_out, 0] * centre[:, 0]
        for field_in in range(1, centre.shape[1]):
            running = running + coefficients[field_out, field_in] * centre[:, field_in]
        outputs.append(running)
    return jnp.stack(outputs, axis=1)

def reference(pod_modes, velocity, region, partner, coupling_table):
    mode_count = pod_modes.shape[0]
    fields = pod_modes.shape[1]
    off_diagonal = 1.0 - jnp.eye(fields, dtype=jnp.float32)
    masked = coupling_table * off_diagonal[None]
    last_plane = NX - 1

    def plane_step(plane_index, summed):
        centre = lax.dynamic_index_in_dim(pod_modes, plane_index, 2, keepdims=False).astype(jnp.float32)
        upper_index = jnp.minimum(plane_index + 1, last_plane)
        lower_index = jnp.maximum(plane_index - 1, 0)
        upper_cells = lax.dynamic_index_in_dim(pod_modes, upper_index, 2, keepdims=False).astype(jnp.float32)
        upper_cells = upper_cells * (plane_index < last_plane).astype(jnp.float32)
        lower_cells = lax.dynamic_index_in_dim(pod_modes, lower_index, 2, keepdims=False).astype(jnp.float32)
        lower_cells = lower_cells * (plane_index > 0).astype(jnp.float32)
        speeds = lax.dynamic_index_in_dim(velocity, plane_index, 1, keepdims=False)
        term_x = speeds[0] * (0.5 * (upper_cells - lower_cells))
        padded = jnp.pad(centre, ((0, 0), (0, 0), (1, 1), (0, 0)))
        term_y = speeds[1] * (0.5 * (padded[:, :, 2:] - padded[:, :, :-2]))
        term_z = speeds[2] * (jnp.take(centre, partner, axis=3) - centre)
        labels = lax.dynamic_index_in_dim(region, plane_index, 0, keepdims=False)
        coefficients = jnp.moveaxis(masked[labels], (2, 3), (0, 1))
        term_c = coupling_terms(centre, coefficients)
        flattened = centre.reshape(mode_count, -1)
        outputs = []
        for operator_term in (term_x, term_y, term_z, term_c):
            rounded = operator_term.astype(jnp.bfloat16)
            rounded = lax.optimization_barrier(rounded).astype(jnp.float32)
            outputs.append(jnp.einsum('ik,jk->ij', flattened, rounded.reshape(mode_count, -1)))
        return summed + jnp.stack(outputs)
    summed = lax.fori_loop(0, NX, plane_step, jnp.zeros((4, mode_count, mode_count), jnp.float32))
    return summed * (1.0 / math.sqrt(FIELDS * NX * NY * NZ))
```

```python
import math

import jax
import jax.numpy as jnp
from jax import lax
from jax.sharding import PartitionSpec as P


def extended(cells, sides, width):
    for axis, dim in sides:
        count = lax.axis_size(axis)
        ends = count - 1
        head = lax.slice_in_dim(cells, 0, width, axis=dim)
        tail = lax.slice_in_dim(cells, cells.shape[dim] - width, cells.shape[dim], axis=dim)
        cells = jnp.concatenate(
            [
                lax.ppermute(tail, axis, [(i, (i + 1) % count) for i in range(ends)]),
                cells,
                lax.ppermute(head, axis, [((i + 1) % count, i) for i in range(ends)]),
            ],
            axis=dim,
        )
    return cells


def coupling_terms(centre, coefficients):
    outputs = []
    for field_out in range(centre.shape[1]):
        running = coefficients[field_out, 0] * centre[:, 0]
        for field_in in range(1, centre.shape[1]):
            running = running + coefficients[field_out, field_in] * centre[:, field_in]
        outputs.append(running)
    return jnp.stack(outputs, axis=1)


def cell_coupling(region, coupling_table):
    fields = coupling_table.shape[1]
    off_diagonal = 1.0 - jnp.eye(fields, dtype=jnp.float32)
    masked = coupling_table * off_diagonal[None]
    coefficients = jnp.zeros((fields, fields) + region.shape, jnp.float32)
    for region_id in range(coupling_table.shape[0]):
        coefficients = jnp.where(
            region[None, None] == region_id, masked[region_id][:, :, None, None, None], coefficients
        )
    return coefficients


def face_terms(padded, speeds, coefficients):
    centre = padded[:, :, 1:-1, 1:-1].astype(jnp.float32)
    upper_cells = padded[:, :, 2:, 1:-1].astype(jnp.float32)
    lower_cells = padded[:, :, :-2, 1:-1].astype(jnp.float32)
    term_x = speeds[0] * (0.5 * (upper_cells - lower_cells))
    right_cells = padded[:, :, 1:-1, 2:].astype(jnp.float32)
    left_cells = padded[:, :, 1:-1, :-2].astype(jnp.float32)
    term_y = speeds[1] * (0.5 * (right_cells - left_cells))
    term_c = coupling_terms(centre, coefficients)
    return (term_x.astype(jnp.bfloat16), term_y.astype(jnp.bfloat16), term_c.astype(jnp.bfloat16))


def jump_term(block, speed_z, partner):
    centre = block.astype(jnp.float32)
    return (speed_z * (jnp.take(centre, partner, axis=4) - centre)).astype(jnp.bfloat16)


def summed_over_cells(partial_sums, shares, scaling):
    terms, columns, rows = partial_sums.shape
    lanes = 128
    pieces = partial_sums.reshape(terms, columns, rows // lanes, lanes).transpose(2, 0, 1, 3)
    pieces = pieces.reshape(shares, -1, lanes).astype(jnp.bfloat16)
    received = lax.all_to_all(pieces, ("gx", "gy"), 0, 0)
    share = jnp.sum(received.astype(jnp.float32), axis=0) * scaling
    spread = jnp.broadcast_to(share.astype(jnp.bfloat16)[None], received.shape)
    whole = lax.all_to_all(spread, ("gx", "gy"), 0, 0)
    whole = whole.reshape(rows // lanes, terms, columns, lanes).transpose(1, 0, 3, 2)
    return whole.reshape(terms, rows, columns).astype(jnp.float32)


def on_device(pod_modes, velocity, region, partner, coupling_table):
    blocks, fields, cells_x, cells_y, planes = pod_modes.shape
    cell_total = fields * cells_x * lax.axis_size("gx") * cells_y * lax.axis_size("gy") * planes
    scaling = 1.0 / math.sqrt(cell_total)
    coefficients = cell_coupling(region, coupling_table)
    padded = extended(pod_modes, (("gx", 2), ("gy", 3)), 1)
    image_x, image_y, image_c = face_terms(padded, velocity, coefficients)
    jump_images = jump_term(pod_modes, velocity[2], partner)
    stacked = jnp.stack((image_x, image_y, jump_images, image_c)).reshape(4, blocks, -1)
    portion = lax.all_gather(pod_modes, "ma", axis=0, tiled=True)
    flattened = portion.reshape(portion.shape[0], -1)
    shares = lax.axis_size("gx") * lax.axis_size("gy")
    partial_sums = jnp.einsum("qjk,ik->qji", stacked, flattened, preferred_element_type=jnp.float32)
    return summed_over_cells(partial_sums, shares, scaling)


def solution(mesh):
    placed = (
        P("ma", None, "gx", "gy", None),
        P(None, "gx", "gy", None),
        P("gx", "gy", None),
        P(),
        P(),
    )
    return jax.shard_map(
        on_device, mesh=mesh, in_specs=placed, out_specs=P(None, None, "ma"), check_vma=False
    )
```

```python
import math

import jax
import jax.numpy as jnp
from jax import lax
from jax.experimental import pallas as pl
from jax.experimental.pallas import tpu as pltpu
from jax.sharding import Mesh, PartitionSpec as P

LANES = 128
BF16 = jnp.bfloat16
F32 = jnp.float32
CONTRACT_LAST = (((1,), (1,)), ((), ()))


def shift(cells, axis, step, count):
    return lax.ppermute(cells, axis, [(i, (i + step) % count) for i in range(count)])


def by_pair(cells, swap):
    return jnp.where(swap, cells[::-1], cells)


def local_kernel(table, partner, cells, a, out, modes, z_image, c_image):
    pairs, fields, block = a.shape[0] // 4, a.shape[2], a.shape[3]
    planes = lax.broadcasted_iota(jnp.int32, (LANES, LANES), 0)
    pick = (planes == partner[...]).astype(F32).astype(BF16)
    speed_z, region = cells[0], cells[1]
    coupling = {}
    for f in range(fields):
        for g in range(fields):
            if f != g:
                chosen = jnp.zeros_like(region)
                for number in range(table.shape[0]):
                    chosen = jnp.where(region == float(number), table[number, f * fields + g], chosen)
                coupling[f, g] = chosen
    for p in range(pairs):
        for xi in range(2):
            col = 2 * p + xi
            for j in range(4):
                rows = slice(j * block, (j + 1) * block)
                here = [a[4 * p + j, xi, f] for f in range(fields)]
                moved = jnp.dot(jnp.concatenate(here, axis=0), pick, preferred_element_type=F32)
                centre = [cells_f.astype(F32) for cells_f in here]
                for f in range(fields):
                    chunk = slice((col * fields + f) * LANES, (col * fields + f + 1) * LANES)
                    modes[rows, chunk] = here[f]
                    jump = speed_z[col : col + 1] * (moved[f * block : (f + 1) * block] - centre[f])
                    z_image[rows, chunk] = jump.astype(BF16)
                    running = None
                    for g in range(fields):
                        if g != f:
                            term = coupling[f, g][col : col + 1] * centre[g]
                            running = term if running is None else running + term
                    c_image[rows, chunk] = running.astype(BF16)
    for q, image in enumerate((z_image, c_image)):
        total = lax.dot_general(image[...], modes[...], CONTRACT_LAST, preferred_element_type=F32)
        place(out, q, total, block)


def place(out, q, total, block):
    for j in range(4):
        for half in range(2):
            start = (2 * q + half) * block
            piece = total[j * block : (j + 1) * block, half * LANES : (half + 1) * LANES]
            out[j, start : start + block, :] = piece.astype(BF16)


def edge_kernel(coef, modes, xr, xl, yr, yl, zc, out, x_image, x_edge, x_side, y_image, y_edge, y_side):
    pairs, block = xr.shape[0] // 4, xr.shape[2]
    fields = 2 * xr.shape[1]

    def weight(row):
        return coef[row : row + 1, :]

    for p in range(pairs):
        for j in range(4):
            rows = slice(j * block, (j + 1) * block)
            for f in range(fields):
                def lane_chunk(index):
                    return slice(index * LANES, (index + 1) * LANES)

                first, second = (lane_chunk((2 * p + xi) * fields + f) for xi in range(2))
                side = lane_chunk(p * fields + f)
                m0 = modes[rows, first].astype(F32)
                m1 = modes[rows, second].astype(F32)
                half = f % 2
                to_second = weight(2 * p) * m1
                to_first = -weight(2 * p + 1) * m0
                if f < 2:
                    beside = xr[4 * p + j, half]
                    to_first = weight(4 + p) * beside.astype(F32) + to_first
                    edge = weight(6 + p) * m1
                else:
                    beside = xl[4 * p + j, half]
                    to_second = to_second - weight(8 + p) * beside.astype(F32)
                    edge = weight(10 + p) * m0
                x_image[rows, first] = to_second.astype(BF16)
                x_image[rows, second] = to_first.astype(BF16)
                x_edge[rows, side] = edge.astype(BF16)
                x_side[rows, side] = beside
                for xi, chunk, centre in ((0, first, m0), (1, second, m1)):
                    col = 2 * p + xi
                    next_to = yr[4 * p + j, xi, half] if f < 2 else yl[4 * p + j, xi, half]
                    base = 12 if f < 2 else 20
                    y_image[rows, chunk] = (weight(base + col) * next_to.astype(F32)).astype(BF16)
                    y_edge[rows, chunk] = (weight(base + 4 + col) * centre).astype(BF16)
                    y_side[rows, chunk] = next_to
    for q, (image, edge, side) in enumerate(((x_image, x_edge, x_side), (y_image, y_edge, y_side))):
        total = lax.dot_general(image[...], modes[...], CONTRACT_LAST, preferred_element_type=F32)
        total += lax.dot_general(edge[...], side[...], CONTRACT_LAST, preferred_element_type=F32)
        place(out, q, total, block)
    out[:, 4 * block :, :] = zc[...]


def on_device(pod_modes, velocity, region, partner, coupling_table):
    block, fields, cells_x, cells_y, planes = pod_modes.shape
    zh_count, x_count, gy_count, ma_count = (lax.axis_size(name) for name in ("zh", "x", "gy", "ma"))
    cell_total = fields * cells_x * zh_count * x_count * cells_y * gy_count * planes
    scaling = 1.0 / math.sqrt(cell_total)
    zh, x, gy, ma = (lax.axis_index(name) for name in ("zh", "x", "gy", "ma"))
    row = zh * ma_count + ma
    kinds = block * ma_count

    pieces = jnp.transpose(pod_modes, (3, 2, 1, 0, 4))
    a = lax.all_to_all(pieces, ("zh", "ma"), 0, 0)

    own = jnp.concatenate([velocity, region.astype(F32)[None]])
    other = shift(own, "zh", 1, zh_count)
    cells = jnp.stack([jnp.where(zh == 0, own, other), jnp.where(zh == 0, other, own)], axis=1)
    vx_right = shift(by_pair(cells[0, :, 0], x == 0), "x", -1, x_count)
    vx_left = shift(by_pair(cells[0, :, 1], x == x_count - 1), "x", 1, x_count)
    vy_above = shift(cells[1, :, :, :1], "gy", -1, gy_count)
    vy_below = shift(cells[1, :, :, -1:], "gy", 1, gy_count)
    vy = jnp.concatenate([vy_below, cells[1], vy_above], axis=2).reshape(4, cells_y + 2, planes)
    at_row = lax.dynamic_index_in_dim(cells, row, 3, keepdims=False).reshape(4, 4, planes)
    vx_right = lax.dynamic_index_in_dim(vx_right, row, 1, keepdims=False)
    vx_left = lax.dynamic_index_in_dim(vx_left, row, 1, keepdims=False)
    vy_down, vy_here, vy_up = (lax.dynamic_index_in_dim(vy, row + k, 1, keepdims=False) for k in range(3))
    right = jnp.stack([jnp.ones((), F32), jnp.where(x == x_count - 1, 0.0, 1.0)])[:, None]
    left = jnp.stack([jnp.where(x == 0, 0.0, 1.0), jnp.ones((), F32)])[:, None]
    up = jnp.where((gy == gy_count - 1) & (row == cells_y - 1), 0.0, 1.0)
    down = jnp.where((gy == 0) & (row == 0), 0.0, 1.0)
    vx = at_row[0]
    coef = 0.5 * jnp.concatenate(
        [
            vx,
            vx[1::2] * right,
            -vx_right * right,
            vx[0::2] * left,
            vx_left * left,
            vy_here * up,
            -vy_up * up,
            -vy_here * down,
            vy_down * down,
            jnp.zeros((4, planes), F32),
        ]
    )

    vmem = pl.BlockSpec(memory_space=pltpu.VMEM)
    smem = pl.BlockSpec(memory_space=pltpu.SMEM)
    width = 4 * fields * planes
    wide = pltpu.VMEM((kinds, width), BF16)
    narrow = pltpu.VMEM((kinds, width // 2), BF16)
    zc, modes = pl.pallas_call(
        local_kernel,
        out_shape=(
            jax.ShapeDtypeStruct((ma_count, 4 * block, LANES), BF16),
            jax.ShapeDtypeStruct((kinds, width), BF16),
        ),
        in_specs=[smem, vmem, vmem, vmem],
        out_specs=(vmem, vmem),
        scratch_shapes=[wide, wide],
        compiler_params=pltpu.CompilerParams(vmem_limit_bytes=40 * 2**20),
        cost_estimate=pl.CostEstimate(flops=2 * 2 * kinds * kinds * width, bytes_accessed=4 * 2**20, transcendentals=0),
    )(coupling_table.reshape(-1, fields * fields), partner[None], at_row[2:4], a)

    def pair_swapped(part, swap):
        return by_pair(part.reshape((2, ma_count) + part.shape[1:]), swap).reshape(part.shape)

    def number(grid_row):
        grid_row = grid_row % (gy_count * zh_count * ma_count)
        outer, inner = divmod(grid_row, zh_count * ma_count)
        return (inner // ma_count * gy_count + outer) * ma_count + inner % ma_count

    def row_shift(part, step):
        pairs = [(number(i), number(i + step)) for i in range(gy_count * zh_count * ma_count)]
        return lax.ppermute(part, ("zh", "gy", "ma"), pairs)

    xr = shift(pair_swapped(a[:, 0, :2], x == 0), "x", -1, x_count)
    yr = row_shift(a[:, :, :2], -1)
    xl = shift(pair_swapped(a[:, 1, 2:], x == x_count - 1), "x", 1, x_count)
    yl = row_shift(a[:, :, 2:], 1)

    partial_sums = pl.pallas_call(
        edge_kernel,
        out_shape=jax.ShapeDtypeStruct((ma_count, 8 * block, LANES), BF16),
        in_specs=[vmem] * 7,
        out_specs=vmem,
        scratch_shapes=[wide, narrow, narrow, wide, wide, wide],
        compiler_params=pltpu.CompilerParams(vmem_limit_bytes=40 * 2**20),
        cost_estimate=pl.CostEstimate(flops=2 * 4 * kinds * kinds * width, bytes_accessed=6 * 2**20, transcendentals=0),
    )(coef, modes, xr, xl, yr, yl, zc)

    shares = zh_count * x_count * gy_count
    received = lax.all_to_all(partial_sums.reshape(ma_count * shares, -1, LANES), ("ma", "zh", "x", "gy"), 0, 0)
    share = jnp.sum(received.astype(F32), axis=0) * scaling
    spread = jnp.broadcast_to(share[None], (shares,) + share.shape)
    whole = lax.all_to_all(spread, ("zh", "x", "gy"), 0, 0)
    whole = whole.reshape(4, kinds // LANES, block, LANES).transpose(0, 1, 3, 2)
    return whole.reshape(4, kinds, block)


def solution(mesh):
    gx, gy, ma = (mesh.shape[name] for name in ("gx", "gy", "ma"))
    split = Mesh(mesh.devices.reshape(2, gx // 2, gy, ma), ("zh", "x", "gy", "ma"))
    placed = (
        P("ma", None, ("zh", "x"), "gy", None),
        P(None, ("zh", "x"), "gy", None),
        P(("zh", "x"), "gy", None),
        P(),
        P(),
    )
    return jax.shard_map(
        on_device, mesh=split, in_specs=placed, out_specs=P(None, None, "ma"), check_vma=False
    )
```

```python
import math

import jax
import jax.numpy as jnp
from jax import lax
from jax.experimental import pallas as pl
from jax.experimental.pallas import tpu as pltpu
from jax.sharding import Mesh, PartitionSpec as P

LANES = 128
BF16 = jnp.bfloat16
F32 = jnp.float32
CONTRACT_LAST = (((1,), (1,)), ((), ()))


def steps_along_x(shape, step):
    gx_count, y_count, core_count, ma_count = shape
    half = gx_count // 2
    pairs = []
    for gx in range(gx_count):
        to = gx + step
        if 0 <= to < gx_count:
            for ma in range(ma_count):
                to_ma = ma if gx // half == to // half else ma_count - 1 - ma
                pairs.append((gx * ma_count + ma, to * ma_count + to_ma))
    return pairs


def steps_along_y(shape, step):
    gx_count, y_count, core_count, ma_count = shape
    half = gx_count // 2
    gy_count = y_count * core_count

    def number(gx, place):
        gy, k = divmod(place, ma_count)
        ma = ma_count - 1 - k if (gx // half + gy) % 2 else k
        return (gx * gy_count + gy) * ma_count + ma

    places = gy_count * ma_count
    return [
        (number(gx, place), number(gx, place + step))
        for gx in range(gx_count)
        for place in range(places)
        if 0 <= place + step < places
    ]


def local_kernel(core, table, partner, cells, a, keep, send, modes, z_image, c_image):
    fields, block = a.shape[3], a.shape[4]
    planes = lax.broadcasted_iota(jnp.int32, (LANES, LANES), 0)
    pick = (planes == partner[...]).astype(F32).astype(BF16)
    speed_z, region = cells[0], cells[1]
    coupling = {}
    for f in range(fields):
        for g in range(fields):
            if f != g:
                chosen = jnp.zeros_like(region)
                for number in range(table.shape[0]):
                    chosen = jnp.where(region == float(number), table[number, f * fields + g], chosen)
                coupling[f, g] = chosen
    for col in range(4):
        for j in range(4):
            rows = slice(j * block, (j + 1) * block)
            here = [a[j, col // 2, col % 2, f] for f in range(fields)]
            moved = jnp.dot(jnp.concatenate(here, axis=0), pick, preferred_element_type=F32)
            centre = [cells_f.astype(F32) for cells_f in here]
            for f in range(fields):
                chunk = slice((col * fields + f) * LANES, (col * fields + f + 1) * LANES)
                modes[rows, chunk] = here[f]
                jump = speed_z[col : col + 1] * (moved[f * block : (f + 1) * block] - centre[f])
                z_image[rows, chunk] = jump.astype(BF16)
                running = None
                for g in range(fields):
                    if g != f:
                        term = coupling[f, g][col : col + 1] * centre[g]
                        running = term if running is None else running + term
                c_image[rows, chunk] = running.astype(BF16)
    for q, image in enumerate((z_image, c_image)):
        total = lax.dot_general(image[...], modes[...], CONTRACT_LAST, preferred_element_type=F32)
        place(core, keep, send, q, total, block)


def place(core, keep, send, q, total, block):
    for j in range(4):
        first = total[j * block : (j + 1) * block, :LANES]
        second = total[j * block : (j + 1) * block, LANES:]
        rows = slice(q * block, (q + 1) * block)
        keep[j, rows, :] = jnp.where(core[0] == 0, first, second)
        send[j, rows, :] = jnp.where(core[0] == 0, second, first).astype(BF16)


def edge_kernel(core, coef, modes, xr, xl, yr, yl, zc_keep, zc_send, keep, send, x_image, x_edge, x_side, y_image, y_edge, y_side):
    block, fields = xr.shape[3], 2 * xr.shape[2]

    def weight(row):
        return coef[row : row + 1, :]

    def lane_chunk(index):
        return slice(index * LANES, (index + 1) * LANES)

    axes = (
        (0, xr, xl, x_image, x_edge, x_side, lambda line, end: 2 * line + end),
        (12, yr, yl, y_image, y_edge, y_side, lambda line, end: 2 * end + line),
    )
    for j in range(4):
        rows = slice(j * block, (j + 1) * block)
        for f in range(fields):
            for base, after, before, image, edge, side, col in axes:
                for line in range(2):
                    near, far = (lane_chunk(col(line, end) * fields + f) for end in range(2))
                    extra = lane_chunk(line * fields + f)
                    m0 = modes[rows, near].astype(F32)
                    m1 = modes[rows, far].astype(F32)
                    at_near = weight(base + col(line, 0)) * m1
                    at_far = -weight(base + col(line, 1)) * m0
                    if f < 2:
                        beside = after[j, line, f]
                        at_far = weight(base + 4 + line) * beside.astype(F32) + at_far
                        at_side = weight(base + 6 + line) * m1
                    else:
                        beside = before[j, line, f - 2]
                        at_near = at_near - weight(base + 8 + line) * beside.astype(F32)
                        at_side = weight(base + 10 + line) * m0
                    image[rows, near] = at_near.astype(BF16)
                    image[rows, far] = at_far.astype(BF16)
                    edge[rows, extra] = at_side.astype(BF16)
                    side[rows, extra] = beside
    for q, (_, _, _, image, edge, side, _) in enumerate(axes):
        total = lax.dot_general(image[...], modes[...], CONTRACT_LAST, preferred_element_type=F32)
        total += lax.dot_general(edge[...], side[...], CONTRACT_LAST, preferred_element_type=F32)
        place(core, keep, send, q, total, block)
    keep[:, 2 * block :, :] = zc_keep[...]
    send[:, 2 * block :, :] = zc_send[...]


def on_device(pod_modes, velocity, region, partner, coupling_table):
    block, fields, cells_x, cells_y, planes = pod_modes.shape
    names = ("gx", "y", "core", "ma")
    shape = tuple(lax.axis_size(name) for name in names)
    gx_count, y_count, core_count, ma_count = shape
    gx, y, core, ma = (lax.axis_index(name) for name in names)
    gy_count, gy = y_count * core_count, y * core_count + core
    cell_total = fields * cells_x * gx_count * cells_y * gy_count * planes
    scaling = 1.0 / math.sqrt(cell_total)
    kinds = block * ma_count
    reverse = (gx // (gx_count // 2) + gy) % 2 == 1
    k = jnp.where(reverse, ma_count - 1 - ma, ma)

    pieces = jnp.transpose(pod_modes, (3, 2, 1, 0, 4)).reshape(ma_count, 2, cells_x, fields, block, planes)
    pieces = jnp.where(reverse, pieces[::-1], pieces)
    a = lax.all_to_all(pieces, "ma", 0, 0)

    nothing = 0.0 * pieces[0, 0, 0, 0, 0, :1].astype(F32)
    vx, vy = velocity[0] + nothing, velocity[1] + nothing

    def from_gx(part, step):
        return lax.ppermute(part, "gx", [(i, i + step) for i in range(gx_count) if 0 <= i + step < gx_count])

    def from_gy(part, step):
        pairs = [(i, i + step) for i in range(gy_count) if 0 <= i + step < gy_count]
        return lax.ppermute(part, ("y", "core"), pairs)

    def pair_of(part, axis):
        return lax.dynamic_slice_in_dim(part, 2 * k, 2, axis)

    vx_after = pair_of(from_gx(vx[0], -1), 0)
    vx_before = pair_of(from_gx(vx[-1], 1), 0)
    vy_above = from_gy(vy[:, :1], -1)
    vy_below = from_gy(vy[:, -1:], 1)
    vy_all = jnp.concatenate([vy_below, vy, vy_above], axis=1)
    vy_before = lax.dynamic_index_in_dim(vy_all, 2 * k, 1, keepdims=False)
    vy_after = lax.dynamic_index_in_dim(vy_all, 2 * k + 3, 1, keepdims=False)

    def columns(part):
        return pair_of(part, 1).transpose(1, 0, 2).reshape(4, planes)

    vx, vy = columns(vx), columns(vy)
    right = jnp.where(gx == gx_count - 1, 0.0, 1.0)
    left = jnp.where(gx == 0, 0.0, 1.0)
    up = jnp.where((gy == gy_count - 1) & (k == ma_count - 1), 0.0, 1.0)
    down = jnp.where((gy == 0) & (k == 0), 0.0, 1.0)
    coef = 0.5 * jnp.concatenate(
        [
            vx,
            vx[1::2] * right,
            -vx_after * right,
            vx[0::2] * left,
            vx_before * left,
            vy,
            vy[2:] * up,
            -vy_after * up,
            vy[:2] * down,
            vy_before * down,
        ]
    )
    cells = jnp.stack([columns(velocity[2]), columns(region.astype(F32))])

    vmem = pl.BlockSpec(memory_space=pltpu.VMEM)
    smem = pl.BlockSpec(memory_space=pltpu.SMEM)
    width = 4 * fields * planes
    wide = pltpu.VMEM((kinds, width), BF16)
    narrow = pltpu.VMEM((kinds, width // 2), BF16)

    def sums(terms):
        rows = (ma_count, terms * block, LANES)
        return jax.ShapeDtypeStruct(rows, F32), jax.ShapeDtypeStruct(rows, BF16)

    params = pltpu.CompilerParams(vmem_limit_bytes=40 * 2**20)
    core_here = core.astype(jnp.int32)[None]
    zc_keep, zc_send, modes = pl.pallas_call(
        local_kernel,
        out_shape=(*sums(2), jax.ShapeDtypeStruct((kinds, width), BF16)),
        in_specs=[smem, smem, vmem, vmem, vmem],
        out_specs=(vmem, vmem, vmem),
        scratch_shapes=[wide, wide],
        compiler_params=params,
        cost_estimate=pl.CostEstimate(flops=2 * 2 * kinds * kinds * width, bytes_accessed=4 * 2**20, transcendentals=0),
    )(core_here, coupling_table.reshape(-1, fields * fields), partner[None], cells, a)

    def along_x(part, step):
        return lax.ppermute(part, ("gx", "ma"), steps_along_x(shape, step))

    def along_y(part, step):
        return lax.ppermute(part, names, steps_along_y(shape, step))

    yr = along_y(a[:, 0, :, :2], -1)
    yl = along_y(a[:, 1, :, 2:], 1)
    xr = along_x(a[:, :, 0, :2], -1)
    xl = along_x(a[:, :, 1, 2:], 1)

    keep, send = pl.pallas_call(
        edge_kernel,
        out_shape=sums(4),
        in_specs=[smem] + [vmem] * 8,
        out_specs=(vmem, vmem),
        scratch_shapes=[wide, narrow, narrow, wide, narrow, narrow],
        compiler_params=params,
        cost_estimate=pl.CostEstimate(flops=2 * 3 * kinds * kinds * width, bytes_accessed=6 * 2**20, transcendentals=0),
    )(core_here, coef, modes, xr, xl, yr, yl, zc_keep, zc_send)

    def core_swap(part):
        return lax.ppermute(part, "core", [(i, 1 - i) for i in range(core_count)])

    shares = gx_count * y_count
    both = (keep + core_swap(send).astype(F32)).astype(BF16).reshape(ma_count * shares, -1, LANES)
    received = lax.all_to_all(both, ("ma", "gx", "y"), 0, 0)
    share = jnp.sum(received.astype(F32), axis=0) * scaling
    spread = jnp.broadcast_to(share[None], (shares,) + share.shape)
    mine = lax.all_to_all(spread, ("gx", "y"), 0, 0).reshape(4, block, LANES)
    other = core_swap(mine)
    halves = [jnp.where(core == 0, mine, other), jnp.where(core == 0, other, mine)]
    return jnp.concatenate(halves, axis=2).transpose(0, 2, 1)


def solution(mesh):
    gx, gy, ma = (mesh.shape[name] for name in ("gx", "gy", "ma"))
    split = Mesh(mesh.devices.reshape(gx, gy // 2, 2, ma), ("gx", "y", "core", "ma"))
    placed = (
        P("ma", None, "gx", ("y", "core"), None),
        P(None, "gx", ("y", "core"), None),
        P("gx", ("y", "core"), None),
        P(),
        P(),
    )
    return jax.shard_map(
        on_device, mesh=split, in_specs=placed, out_specs=P(None, None, "ma"), check_vma=False
    )
```

```python
import functools
import math

import jax
import jax.numpy as jnp
from jax import lax
from jax.experimental import pallas as pl
from jax.experimental.pallas import tpu as pltpu
from jax.sharding import Mesh, PartitionSpec as P

LANES = 128
BF16 = jnp.bfloat16
F32 = jnp.float32
CONTRACT_LAST = (((1,), (1,)), ((), ()))


def steps_along_x(shape, step):
    gx_count, y_count, core_count, ma_count = shape
    half = gx_count // 2
    pairs = []
    for gx in range(gx_count):
        to = gx + step
        if 0 <= to < gx_count:
            for ma in range(ma_count):
                to_ma = ma if gx // half == to // half else ma_count - 1 - ma
                pairs.append((gx * ma_count + ma, to * ma_count + to_ma))
    return pairs


def steps_along_y(shape, step):
    gx_count, y_count, core_count, ma_count = shape
    half = gx_count // 2
    gy_count = y_count * core_count

    def number(gx, place):
        gy, k = divmod(place, ma_count)
        ma = ma_count - 1 - k if (gx // half + gy) % 2 else k
        return (gx * gy_count + gy) * ma_count + ma

    places = gy_count * ma_count
    return [
        (number(gx, place), number(gx, place + step))
        for gx in range(gx_count)
        for place in range(places)
        if 0 <= place + step < places
    ]


def pack_kernel(wanted, pieces, *outs):
    half = pieces.shape[3] // 2
    for t in range(4):
        outs[t][...] = pieces[wanted[t], :, :, :half]
        outs[4 + t][...] = pieces[wanted[t], :, :, half:]


def local_kernel(place_of, table, partner, cells, *refs):
    parts, (keep, send, modes, z_image, c_image) = refs[:8], refs[8:]
    fields, block = 2 * parts[0].shape[2], parts[0].shape[3]
    planes = lax.broadcasted_iota(jnp.int32, (LANES, LANES), 0)
    pick = (planes == partner[...]).astype(F32).astype(BF16)
    speed_z, region = cells[0], cells[1]
    coupling = {}
    for f in range(fields):
        for g in range(fields):
            if f != g:
                chosen = jnp.zeros_like(region)
                for number in range(table.shape[0]):
                    chosen = jnp.where(region == float(number), table[number, f * fields + g], chosen)
                coupling[f, g] = chosen
    for col in range(4):
        for t in range(4):
            rows = pl.ds(pl.multiple_of((place_of[1] ^ t) * block, block), block)
            here = [part[col // 2, col % 2, f] for part in (parts[t], parts[4 + t]) for f in range(fields // 2)]
            moved = jnp.dot(jnp.concatenate(here, axis=0), pick, preferred_element_type=F32)
            centre = [cells_f.astype(F32) for cells_f in here]
            for f in range(fields):
                chunk = slice((col * fields + f) * LANES, (col * fields + f + 1) * LANES)
                modes[rows, chunk] = here[f]
                jump = speed_z[col : col + 1] * (moved[f * block : (f + 1) * block] - centre[f])
                z_image[rows, chunk] = jump.astype(BF16)
                running = None
                for g in range(fields):
                    if g != f:
                        term = coupling[f, g][col : col + 1] * centre[g]
                        running = term if running is None else running + term
                c_image[rows, chunk] = running.astype(BF16)
    for q, image in enumerate((z_image, c_image)):
        total = lax.dot_general(image[...], modes[...], CONTRACT_LAST, preferred_element_type=F32)
        place(place_of, keep, send, q, total, block)


def place(place_of, keep, send, q, total, block):
    for j in range(4):
        first = total[j * block : (j + 1) * block, :LANES]
        second = total[j * block : (j + 1) * block, LANES:]
        rows = slice(q * block, (q + 1) * block)
        keep[j, rows, :] = jnp.where(place_of[0] == 0, first, second)
        send[j, rows, :] = jnp.where(place_of[0] == 0, second, first).astype(BF16)


def edge_kernel(place_of, speeds, modes, xr, xl, yr, yl, zc_keep, zc_send, keep, send, x_image, x_edge, x_side, y_image, y_edge, y_side):
    fields, block = 4, modes.shape[0] // 4
    body = 4 * fields * block
    half_speeds = 0.5 * speeds[...]

    def beside_speeds(message):
        rows = message[body:, :].astype(F32)
        return 0.5 * (rows[0:2] + rows[2:4] + rows[4:6])

    def lane_chunk(index):
        return slice(index * LANES, (index + 1) * LANES)

    axes = (
        (0, xr, xl, x_image, x_edge, x_side, lambda line, end: 2 * line + end),
        (4, yr, yl, y_image, y_edge, y_side, lambda line, end: 2 * end + line),
    )
    for base, after, before, image, edge, side, col in axes:
        after_speeds, before_speeds = beside_speeds(after), beside_speeds(before)
        for line in range(2):
            near_speed = half_speeds[base + col(line, 0) : base + col(line, 0) + 1]
            far_speed = half_speeds[base + col(line, 1) : base + col(line, 1) + 1]
            after_speed = after_speeds[line : line + 1]
            before_speed = before_speeds[line : line + 1]
            for j in range(4):
                rows = slice(j * block, (j + 1) * block)
                for f in range(fields):
                    near, far = (lane_chunk(col(line, end) * fields + f) for end in range(2))
                    extra = lane_chunk(line * fields + f)
                    m0 = modes[rows, near].astype(F32)
                    m1 = modes[rows, far].astype(F32)
                    at_near = near_speed * m1
                    at_far = -far_speed * m0
                    start = ((2 * j + line) * 2 + f % 2) * block
                    if f < 2:
                        beside = after[start : start + block, :]
                        at_far = far_speed * beside.astype(F32) + at_far
                        at_side = -after_speed * m1
                    else:
                        beside = before[start : start + block, :]
                        at_near = at_near - near_speed * beside.astype(F32)
                        at_side = before_speed * m0
                    image[rows, near] = at_near.astype(BF16)
                    image[rows, far] = at_far.astype(BF16)
                    edge[rows, extra] = at_side.astype(BF16)
                    side[rows, extra] = beside
    for q, (_, _, _, image, edge, side, _) in enumerate(axes):
        total = lax.dot_general(image[...], modes[...], CONTRACT_LAST, preferred_element_type=F32)
        total += lax.dot_general(edge[...], side[...], CONTRACT_LAST, preferred_element_type=F32)
        place(place_of, keep, send, q, total, block)
    keep[:, 2 * block :, :] = zc_keep[...]
    send[:, 2 * block :, :] = zc_send[...]


def message_kernel(end, place_of, speeds, *refs):
    parts, (x_message, y_message) = refs[:4], refs[4:]
    block = parts[0].shape[3]
    body = 16 * block
    vx, vy = speeds[:4], speeds[4:]
    for t in range(4):
        for line in range(2):
            for f in range(2):
                start = ((place_of[1] ^ t) * 4 + line * 2 + f) * block
                rows = pl.ds(pl.multiple_of(start, block), block)
                x_message[rows, :] = parts[t][line, end, f]
                y_message[rows, :] = parts[t][end, line, f]
    for message, at_edge in (
        (x_message, jnp.concatenate([vx[end : end + 1], vx[2 + end : 3 + end]])),
        (y_message, vy[2 * end : 2 * end + 2]),
    ):
        first = at_edge.astype(BF16).astype(F32)
        rest = at_edge - first
        second = rest.astype(BF16).astype(F32)
        third = rest - second
        message[body:, :] = jnp.concatenate([first, second, third, jnp.zeros((10, LANES), F32)]).astype(BF16)


def on_device(pod_modes, velocity, region, partner, coupling_table):
    block, fields, cells_x, cells_y, planes = pod_modes.shape
    names = ("gx", "y", "core", "ma")
    shape = tuple(lax.axis_size(name) for name in names)
    gx_count, y_count, core_count, ma_count = shape
    gx, y, core, ma = (lax.axis_index(name) for name in names)
    gy_count, gy = y_count * core_count, y * core_count + core
    cell_total = fields * cells_x * gx_count * cells_y * gy_count * planes
    scaling = 1.0 / math.sqrt(cell_total)
    kinds = block * ma_count
    reverse = (gx // (gx_count // 2) + gy) % 2 == 1
    k = jnp.where(reverse, ma_count - 1 - ma, ma)

    homes = jnp.stack([ma ^ t for t in range(ma_count)])
    wanted = jnp.where(reverse, ma_count - 1 - homes, homes).astype(jnp.int32)
    vmem = pl.BlockSpec(memory_space=pltpu.VMEM)
    smem = pl.BlockSpec(memory_space=pltpu.SMEM)
    params = pltpu.CompilerParams(vmem_limit_bytes=40 * 2**20)
    pieces = jnp.transpose(pod_modes, (3, 2, 1, 0, 4)).reshape(ma_count, 2, cells_x, fields, block, planes)
    piece = jax.ShapeDtypeStruct((2, cells_x, fields // 2, block, planes), BF16)
    packed = pl.pallas_call(
        pack_kernel,
        out_shape=(piece,) * (2 * ma_count),
        in_specs=[smem, vmem],
        out_specs=(vmem,) * (2 * ma_count),
        compiler_params=params,
        cost_estimate=pl.CostEstimate(flops=0, bytes_accessed=2 * 2**20, transcendentals=0),
    )(wanted, pieces)

    def collected(parts):
        blocks = {0: parts[0]}
        for t in (2, 3, 1):
            blocks[t] = lax.ppermute(parts[t], "ma", [(i, i ^ t) for i in range(ma_count)])
        return [blocks[t] for t in range(ma_count)]

    low, high = collected(packed[:ma_count]), collected(packed[ma_count:])

    def columns(part):
        return lax.dynamic_slice_in_dim(part, 2 * k, 2, 1).transpose(1, 0, 2).reshape(4, planes)

    vx, vy = columns(velocity[0]), columns(velocity[1])
    cells = jnp.stack([columns(velocity[2]), columns(region.astype(F32))])

    speeds = jnp.concatenate([vx, vy])
    place_of = jnp.stack([core, ma]).astype(jnp.int32)
    width = 4 * fields * planes
    wide = pltpu.VMEM((kinds, width), BF16)
    narrow = pltpu.VMEM((kinds, width // 2), BF16)

    def sums(terms):
        rows = (ma_count, terms * block, LANES)
        return jax.ShapeDtypeStruct(rows, F32), jax.ShapeDtypeStruct(rows, BF16)

    zc_keep, zc_send, modes = pl.pallas_call(
        local_kernel,
        out_shape=(*sums(2), jax.ShapeDtypeStruct((kinds, width), BF16)),
        in_specs=[smem, smem] + [vmem] * 10,
        out_specs=(vmem, vmem, vmem),
        scratch_shapes=[wide, wide],
        compiler_params=params,
        cost_estimate=pl.CostEstimate(flops=2 * 2 * kinds * kinds * width, bytes_accessed=4 * 2**20, transcendentals=0),
    )(place_of, coupling_table.reshape(-1, fields * fields), partner[None], cells, *low, *high)

    def messages(parts, end):
        rows = jax.ShapeDtypeStruct((4 * fields * block + 16, LANES), BF16)
        return pl.pallas_call(
            functools.partial(message_kernel, end),
            out_shape=(rows, rows),
            in_specs=[smem] + [vmem] * 5,
            out_specs=(vmem, vmem),
            compiler_params=params,
            cost_estimate=pl.CostEstimate(flops=0, bytes_accessed=2**20, transcendentals=0),
        )(place_of, speeds, *parts)

    def along_x(part, step):
        return lax.ppermute(part, ("gx", "ma"), steps_along_x(shape, step))

    def along_y(part, step):
        return lax.ppermute(part, names, steps_along_y(shape, step))

    x_message, y_message = messages(low, 0)
    xr, yr = along_x(x_message, -1), along_y(y_message, -1)
    x_message, y_message = messages(high, 1)
    xl, yl = along_x(x_message, 1), along_y(y_message, 1)

    keep, send = pl.pallas_call(
        edge_kernel,
        out_shape=sums(4),
        in_specs=[smem] + [vmem] * 8,
        out_specs=(vmem, vmem),
        scratch_shapes=[wide, narrow, narrow, wide, narrow, narrow],
        compiler_params=params,
        cost_estimate=pl.CostEstimate(flops=2 * 3 * kinds * kinds * width, bytes_accessed=6 * 2**20, transcendentals=0),
    )(place_of, speeds, modes, xr, xl, yr, yl, zc_keep, zc_send)

    def core_swap(part):
        return lax.ppermute(part, "core", [(i, 1 - i) for i in range(core_count)])

    shares = gx_count * y_count
    both = (keep + core_swap(send).astype(F32)).astype(BF16).reshape(ma_count * shares, -1, LANES)
    received = lax.all_to_all(both, ("ma", "gx", "y"), 0, 0)
    share = jnp.sum(received.astype(F32), axis=0) * scaling
    spread = jnp.broadcast_to(share[None], (shares,) + share.shape)
    mine = lax.all_to_all(spread, ("gx", "y"), 0, 0).reshape(4, block, LANES)
    other = core_swap(mine)
    halves = [jnp.where(core == 0, mine, other), jnp.where(core == 0, other, mine)]
    return jnp.concatenate(halves, axis=2).transpose(0, 2, 1)


def solution(mesh):
    gx, gy, ma = (mesh.shape[name] for name in ("gx", "gy", "ma"))
    split = Mesh(mesh.devices.reshape(gx, gy // 2, 2, ma), ("gx", "y", "core", "ma"))
    placed = (
        P("ma", None, "gx", ("y", "core"), None),
        P(None, "gx", ("y", "core"), None),
        P("gx", ("y", "core"), None),
        P(),
        P(),
    )
    return jax.shard_map(
        on_device, mesh=split, in_specs=placed, out_specs=P(None, None, "ma"), check_vma=False
    )
```

```python
import math

import jax
import jax.numpy as jnp
from jax import lax
from jax.experimental import pallas as pl
from jax.experimental.pallas import tpu as pltpu
from jax.sharding import Mesh, PartitionSpec as P

LANES = 128
BF16 = jnp.bfloat16
F32 = jnp.float32
CONTRACT_LAST = (((1,), (1,)), ((), ()))


def steps_along_x(shape, step):
    gx_count, y_count, core_count, ma_count = shape
    half = gx_count // 2
    pairs = []
    for gx in range(gx_count):
        to = gx + step
        if 0 <= to < gx_count:
            for ma in range(ma_count):
                to_ma = ma if gx // half == to // half else ma_count - 1 - ma
                pairs.append((gx * ma_count + ma, to * ma_count + to_ma))
    return pairs


def steps_along_y(shape, step):
    gx_count, y_count, core_count, ma_count = shape
    half = gx_count // 2
    gy_count = y_count * core_count

    def number(gx, place):
        gy, k = divmod(place, ma_count)
        ma = ma_count - 1 - k if (gx // half + gy) % 2 else k
        return (gx * gy_count + gy) * ma_count + ma

    places = gy_count * ma_count
    return [
        (number(gx, place), number(gx, place + step))
        for gx in range(gx_count)
        for place in range(places)
        if 0 <= place + step < places
    ]


def pack_kernel(wanted, pieces, *outs):
    for t in range(4):
        outs[t][0] = pieces[wanted[t], 0, 1]
        outs[t][1] = pieces[wanted[t], 1, 0]
        outs[4][t, 0] = pieces[wanted[4 + t], 0, 0]
        outs[4][t, 1] = pieces[wanted[4 + t], 1, 1]


def local_kernel(place_of, table, partner, cells, *refs):
    early, late, (keep, send, modes, z_image, c_image) = refs[:4], refs[4], refs[5:]
    fields, block = late.shape[2], late.shape[3]
    planes = lax.broadcasted_iota(jnp.int32, (LANES, LANES), 0)
    pick = (planes == partner[...]).astype(F32).astype(BF16)
    speed_z, region = cells[0], cells[1]
    coupling = {}
    for f in range(fields):
        for g in range(fields):
            if f != g:
                chosen = jnp.zeros_like(region)
                for number in range(table.shape[0]):
                    chosen = jnp.where(region == float(number), table[number, f * fields + g], chosen)
                coupling[f, g] = chosen
    for col in range(4):
        for t in range(4):
            if col in (0, 3):
                rows = slice(t * block, (t + 1) * block)
                here = [late[t, col // 2, f] for f in range(fields)]
            else:
                rows = pl.ds(pl.multiple_of((place_of[1] ^ t) * block, block), block)
                here = [early[t][col - 1, f] for f in range(fields)]
            moved = jnp.dot(jnp.concatenate(here, axis=0), pick, preferred_element_type=F32)
            centre = [cells_f.astype(F32) for cells_f in here]
            for f in range(fields):
                chunk = slice((col * fields + f) * LANES, (col * fields + f + 1) * LANES)
                modes[rows, chunk] = here[f]
                jump = speed_z[col : col + 1] * (moved[f * block : (f + 1) * block] - centre[f])
                z_image[rows, chunk] = jump.astype(BF16)
                running = None
                for g in range(fields):
                    if g != f:
                        term = coupling[f, g][col : col + 1] * centre[g]
                        running = term if running is None else running + term
                c_image[rows, chunk] = running.astype(BF16)
    for q, image in enumerate((z_image, c_image)):
        total = lax.dot_general(image[...], modes[...], CONTRACT_LAST, preferred_element_type=F32)
        place(place_of, keep, send, q, total, block)


def place(place_of, keep, send, q, total, block):
    for j in range(4):
        first = total[j * block : (j + 1) * block, :LANES]
        second = total[j * block : (j + 1) * block, LANES:]
        rows = slice(q * block, (q + 1) * block)
        keep[j, rows, :] = jnp.where(place_of[0] == 0, first, second)
        send[j, rows, :] = jnp.where(place_of[0] == 0, second, first).astype(BF16)


def edge_kernel(place_of, speeds, modes, xr, xl, yr, yl, zc_keep, zc_send, keep, send, x_image, x_edge, x_side, y_image, y_edge, y_side):
    fields, block = 4, modes.shape[0] // 4
    body = 4 * fields * block
    half_speeds = 0.5 * speeds[...]

    def beside_speed(message, axis):
        rows = message[body:, :].astype(F32)[3 * axis : 3 * axis + 3]
        return 0.5 * (rows[0:1] + rows[1:2] + rows[2:3])

    def lane_chunk(index):
        return slice(index * LANES, (index + 1) * LANES)

    axes = (
        (0, xr, xl, x_image, x_edge, x_side, lambda line, end: 2 * line + end),
        (4, yr, yl, y_image, y_edge, y_side, lambda line, end: 2 * end + line),
    )
    for axis, (base, after, before, image, edge, side, col) in enumerate(axes):
        for line, message in enumerate((before, after)):
            near_speed = half_speeds[base + col(line, 0) : base + col(line, 0) + 1]
            far_speed = half_speeds[base + col(line, 1) : base + col(line, 1) + 1]
            their_speed = beside_speed(message, axis)
            for j in range(4):
                rows = slice(j * block, (j + 1) * block)
                for f in range(fields):
                    near, far = (lane_chunk(col(line, end) * fields + f) for end in range(2))
                    extra = lane_chunk(line * fields + f)
                    m0 = modes[rows, near].astype(F32)
                    m1 = modes[rows, far].astype(F32)
                    start = (j * fields + f) * block
                    beside = message[start : start + block, :]
                    at_near = near_speed * m1
                    at_far = -far_speed * m0
                    if line == 1:
                        at_far = far_speed * beside.astype(F32) + at_far
                        at_side = -their_speed * m1
                    else:
                        at_near = at_near - near_speed * beside.astype(F32)
                        at_side = their_speed * m0
                    image[rows, near] = at_near.astype(BF16)
                    image[rows, far] = at_far.astype(BF16)
                    edge[rows, extra] = at_side.astype(BF16)
                    side[rows, extra] = beside
    for q, (_, _, _, image, edge, side, _) in enumerate(axes):
        total = lax.dot_general(image[...], modes[...], CONTRACT_LAST, preferred_element_type=F32)
        total += lax.dot_general(edge[...], side[...], CONTRACT_LAST, preferred_element_type=F32)
        place(place_of, keep, send, q, total, block)
    keep[:, 2 * block :, :] = zc_keep[...]
    send[:, 2 * block :, :] = zc_send[...]


def message_kernel(place_of, speeds, *refs):
    parts, messages = refs[:4], refs[4:]
    fields, block = parts[0].shape[1], parts[0].shape[2]
    body = 4 * fields * block
    for number, message in enumerate(messages):
        for t in range(4):
            for f in range(fields):
                start = ((place_of[1] ^ t) * fields + f) * block
                message[pl.ds(pl.multiple_of(start, block), block), :] = parts[t][number, f]
        rows = []
        for axis in range(2):
            rest = speeds[4 * axis + 1 + number : 4 * axis + 2 + number, :]
            for _ in range(3):
                rows.append(rest.astype(BF16).astype(F32))
                rest = rest - rows[-1]
        rows.append(jnp.zeros((10, LANES), F32))
        message[body:, :] = jnp.concatenate(rows).astype(BF16)


def on_device(pod_modes, velocity, region, partner, coupling_table):
    block, fields, cells_x, cells_y, planes = pod_modes.shape
    names = ("gx", "y", "core", "ma")
    shape = tuple(lax.axis_size(name) for name in names)
    gx_count, y_count, core_count, ma_count = shape
    gx, y, core, ma = (lax.axis_index(name) for name in names)
    gy_count, gy = y_count * core_count, y * core_count + core
    cell_total = fields * cells_x * gx_count * cells_y * gy_count * planes
    scaling = 1.0 / math.sqrt(cell_total)
    kinds = block * ma_count
    reverse = (gx // (gx_count // 2) + gy) % 2 == 1
    k = jnp.where(reverse, ma_count - 1 - ma, ma)

    homes = jnp.stack([ma ^ t for t in range(ma_count)] + [jnp.asarray(m) for m in range(ma_count)])
    wanted = jnp.where(reverse, ma_count - 1 - homes, homes).astype(jnp.int32)
    vmem = pl.BlockSpec(memory_space=pltpu.VMEM)
    smem = pl.BlockSpec(memory_space=pltpu.SMEM)
    params = pltpu.CompilerParams(vmem_limit_bytes=40 * 2**20)
    pieces = jnp.transpose(pod_modes, (3, 2, 1, 0, 4)).reshape(ma_count, 2, cells_x, fields, block, planes)
    piece = (2, fields, block, planes)
    *early, late = pl.pallas_call(
        pack_kernel,
        out_shape=(jax.ShapeDtypeStruct(piece, BF16),) * ma_count + (jax.ShapeDtypeStruct((ma_count, *piece), BF16),),
        in_specs=[smem, vmem],
        out_specs=(vmem,) * (ma_count + 1),
        compiler_params=params,
        cost_estimate=pl.CostEstimate(flops=0, bytes_accessed=2 * 2**20, transcendentals=0),
    )(wanted, pieces)
    for t in (2, 3, 1):
        early[t] = lax.ppermute(early[t], "ma", [(i, i ^ t) for i in range(ma_count)])
    late = lax.all_to_all(late, "ma", 0, 0)

    def columns(part):
        return lax.dynamic_slice_in_dim(part, 2 * k, 2, 1).transpose(1, 0, 2).reshape(4, planes)

    vx, vy = columns(velocity[0]), columns(velocity[1])
    cells = jnp.stack([columns(velocity[2]), columns(region.astype(F32))])

    speeds = jnp.concatenate([vx, vy])
    place_of = jnp.stack([core, ma]).astype(jnp.int32)
    width = 4 * fields * planes
    wide = pltpu.VMEM((kinds, width), BF16)
    narrow = pltpu.VMEM((kinds, width // 2), BF16)

    def sums(terms):
        rows = (ma_count, terms * block, LANES)
        return jax.ShapeDtypeStruct(rows, F32), jax.ShapeDtypeStruct(rows, BF16)

    zc_keep, zc_send, modes = pl.pallas_call(
        local_kernel,
        out_shape=(*sums(2), jax.ShapeDtypeStruct((kinds, width), BF16)),
        in_specs=[smem, smem] + [vmem] * 7,
        out_specs=(vmem, vmem, vmem),
        scratch_shapes=[wide, wide],
        compiler_params=params,
        cost_estimate=pl.CostEstimate(flops=2 * 2 * kinds * kinds * width, bytes_accessed=4 * 2**20, transcendentals=0),
    )(place_of, coupling_table.reshape(-1, fields * fields), partner[None], cells, *early, late)

    rows = jax.ShapeDtypeStruct((4 * fields * block + 16, LANES), BF16)
    first, second = pl.pallas_call(
        message_kernel,
        out_shape=(rows, rows),
        in_specs=[smem] + [vmem] * 5,
        out_specs=(vmem, vmem),
        compiler_params=params,
        cost_estimate=pl.CostEstimate(flops=0, bytes_accessed=2**20, transcendentals=0),
    )(place_of, speeds, *early)

    def along_x(part, step):
        return lax.ppermute(part, ("gx", "ma"), steps_along_x(shape, step))

    def along_y(part, step):
        return lax.ppermute(part, names, steps_along_y(shape, step))

    xr, xl = along_x(second, -1), along_x(first, 1)
    yr, yl = along_y(first, -1), along_y(second, 1)

    keep, send = pl.pallas_call(
        edge_kernel,
        out_shape=sums(4),
        in_specs=[smem] + [vmem] * 8,
        out_specs=(vmem, vmem),
        scratch_shapes=[wide, narrow, narrow, wide, narrow, narrow],
        compiler_params=params,
        cost_estimate=pl.CostEstimate(flops=2 * 3 * kinds * kinds * width, bytes_accessed=6 * 2**20, transcendentals=0),
    )(place_of, speeds, modes, xr, xl, yr, yl, zc_keep, zc_send)

    def core_swap(part):
        return lax.ppermute(part, "core", [(i, 1 - i) for i in range(core_count)])

    shares = gx_count * y_count
    both = (keep + core_swap(send).astype(F32)).astype(BF16).reshape(ma_count * shares, -1, LANES)
    received = lax.all_to_all(both, ("ma", "gx", "y"), 0, 0)
    share = jnp.sum(received.astype(F32), axis=0) * scaling
    spread = jnp.broadcast_to(share[None], (shares * core_count,) + share.shape)
    whole = lax.all_to_all(spread, ("core", "gx", "y"), 0, 0)
    return whole.reshape(core_count, 4, block, LANES).transpose(1, 0, 3, 2).reshape(4, kinds, block)


def solution(mesh):
    gx, gy, ma = (mesh.shape[name] for name in ("gx", "gy", "ma"))
    split = Mesh(mesh.devices.reshape(gx, gy // 2, 2, ma), ("gx", "y", "core", "ma"))
    placed = (
        P("ma", None, "gx", ("y", "core"), None),
        P(None, "gx", ("y", "core"), None),
        P("gx", ("y", "core"), None),
        P(),
        P(),
    )
    return jax.shard_map(
        on_device, mesh=split, in_specs=placed, out_specs=P(None, None, "ma"), check_vma=False
    )
```

```python
import math

import jax
import jax.numpy as jnp
from jax import lax
from jax.experimental import pallas as pl
from jax.experimental.pallas import tpu as pltpu
from jax.sharding import Mesh, PartitionSpec as P

LANES = 128
BF16 = jnp.bfloat16
F32 = jnp.float32
CONTRACT_LAST = (((1,), (1,)), ((), ()))


def steps_along_x(shape, step):
    gx_count, y_count, core_count, ma_count = shape
    half = gx_count // 2
    pairs = []
    for gx in range(gx_count):
        to = gx + step
        if 0 <= to < gx_count:
            for ma in range(ma_count):
                to_ma = ma if gx // half == to // half else ma_count - 1 - ma
                pairs.append((gx * ma_count + ma, to * ma_count + to_ma))
    return pairs


def steps_along_y(shape, step):
    gx_count, y_count, core_count, ma_count = shape
    half = gx_count // 2
    gy_count = y_count * core_count

    def number(gx, place):
        gy, k = divmod(place, ma_count)
        ma = ma_count - 1 - k if (gx // half + gy) % 2 else k
        return (gx * gy_count + gy) * ma_count + ma

    places = gy_count * ma_count
    return [
        (number(gx, place), number(gx, place + step))
        for gx in range(gx_count)
        for place in range(places)
        if 0 <= place + step < places
    ]


def pack_kernel(wanted, pieces, *outs):
    for t in range(4):
        outs[t][...] = pieces[wanted[t]]


def local_kernel(place_of, table, partner, cells, *refs):
    parts, (keep, send, modes, z_image, c_image) = refs[:4], refs[4:]
    fields, block = parts[0].shape[2], parts[0].shape[3]
    planes = lax.broadcasted_iota(jnp.int32, (LANES, LANES), 0)
    pick = (planes == partner[...]).astype(F32).astype(BF16)
    speed_z, region = cells[0], cells[1]
    coupling = {}
    for f in range(fields):
        for g in range(fields):
            if f != g:
                chosen = jnp.zeros_like(region)
                for number in range(table.shape[0]):
                    chosen = jnp.where(region == float(number), table[number, f * fields + g], chosen)
                coupling[f, g] = chosen
    for col in range(4):
        for t in range(4):
            rows = pl.ds(pl.multiple_of((place_of[1] ^ t) * block, block), block)
            here = [parts[t][col // 2, col % 2, f] for f in range(fields)]
            moved = jnp.dot(jnp.concatenate(here, axis=0), pick, preferred_element_type=F32)
            centre = [cells_f.astype(F32) for cells_f in here]
            for f in range(fields):
                chunk = slice((col * fields + f) * LANES, (col * fields + f + 1) * LANES)
                modes[rows, chunk] = here[f]
                jump = speed_z[col : col + 1] * (moved[f * block : (f + 1) * block] - centre[f])
                z_image[rows, chunk] = jump.astype(BF16)
                running = None
                for g in range(fields):
                    if g != f:
                        term = coupling[f, g][col : col + 1] * centre[g]
                        running = term if running is None else running + term
                c_image[rows, chunk] = running.astype(BF16)
    for q, image in enumerate((z_image, c_image)):
        total = lax.dot_general(image[...], modes[...], CONTRACT_LAST, preferred_element_type=F32)
        place(place_of, keep, send, q, total, block)


def place(place_of, keep, send, q, total, block):
    for j in range(4):
        first = total[j * block : (j + 1) * block, :LANES]
        second = total[j * block : (j + 1) * block, LANES:]
        rows = slice(q * block, (q + 1) * block)
        keep[j, rows, :] = jnp.where(place_of[0] == 0, first, second)
        send[j, rows, :] = jnp.where(place_of[0] == 0, second, first).astype(BF16)


def edge_kernel(place_of, speeds, modes, xr, xl, yr, yl, zc_keep, zc_send, keep, send, x_image, x_edge, x_side, y_image, y_edge, y_side):
    fields, block = 4, modes.shape[0] // 4
    body = 4 * fields * block
    half_speeds = 0.5 * speeds[...]

    def beside_speed(message, axis):
        rows = message[body:, :].astype(F32)[3 * axis : 3 * axis + 3]
        return 0.5 * (rows[0:1] + rows[1:2] + rows[2:3])

    def lane_chunk(index):
        return slice(index * LANES, (index + 1) * LANES)

    axes = (
        (0, xr, xl, x_image, x_edge, x_side, lambda line, end: 2 * line + end),
        (4, yr, yl, y_image, y_edge, y_side, lambda line, end: 2 * end + line),
    )
    for axis, (base, after, before, image, edge, side, col) in enumerate(axes):
        for line, message in enumerate((before, after)):
            near_speed = half_speeds[base + col(line, 0) : base + col(line, 0) + 1]
            far_speed = half_speeds[base + col(line, 1) : base + col(line, 1) + 1]
            their_speed = beside_speed(message, axis)
            for j in range(4):
                rows = slice(j * block, (j + 1) * block)
                for f in range(fields):
                    near, far = (lane_chunk(col(line, end) * fields + f) for end in range(2))
                    extra = lane_chunk(line * fields + f)
                    m0 = modes[rows, near].astype(F32)
                    m1 = modes[rows, far].astype(F32)
                    start = (j * fields + f) * block
                    beside = message[start : start + block, :]
                    at_near = near_speed * m1
                    at_far = -far_speed * m0
                    if line == 1:
                        at_far = far_speed * beside.astype(F32) + at_far
                        at_side = -their_speed * m1
                    else:
                        at_near = at_near - near_speed * beside.astype(F32)
                        at_side = their_speed * m0
                    image[rows, near] = at_near.astype(BF16)
                    image[rows, far] = at_far.astype(BF16)
                    edge[rows, extra] = at_side.astype(BF16)
                    side[rows, extra] = beside
    for q, (_, _, _, image, edge, side, _) in enumerate(axes):
        total = lax.dot_general(image[...], modes[...], CONTRACT_LAST, preferred_element_type=F32)
        total += lax.dot_general(edge[...], side[...], CONTRACT_LAST, preferred_element_type=F32)
        place(place_of, keep, send, q, total, block)
    keep[:, 2 * block :, :] = zc_keep[...]
    send[:, 2 * block :, :] = zc_send[...]


def message_kernel(place_of, speeds, *refs):
    parts, messages = refs[:4], refs[4:]
    fields, block = parts[0].shape[2], parts[0].shape[3]
    body = 4 * fields * block
    for number, message in enumerate(messages):
        for t in range(4):
            for f in range(fields):
                start = ((place_of[1] ^ t) * fields + f) * block
                message[pl.ds(pl.multiple_of(start, block), block), :] = parts[t][number, 1 - number, f]
        rows = []
        for axis in range(2):
            rest = speeds[4 * axis + 1 + number : 4 * axis + 2 + number, :]
            for _ in range(3):
                rows.append(rest.astype(BF16).astype(F32))
                rest = rest - rows[-1]
        rows.append(jnp.zeros((10, LANES), F32))
        message[body:, :] = jnp.concatenate(rows).astype(BF16)


def on_device(pod_modes, velocity, region, partner, coupling_table):
    block, fields, cells_x, cells_y, planes = pod_modes.shape
    names = ("gx", "y", "core", "ma")
    shape = tuple(lax.axis_size(name) for name in names)
    gx_count, y_count, core_count, ma_count = shape
    gx, y, core, ma = (lax.axis_index(name) for name in names)
    gy_count, gy = y_count * core_count, y * core_count + core
    cell_total = fields * cells_x * gx_count * cells_y * gy_count * planes
    scaling = 1.0 / math.sqrt(cell_total)
    kinds = block * ma_count
    reverse = (gx // (gx_count // 2) + gy) % 2 == 1
    k = jnp.where(reverse, ma_count - 1 - ma, ma)

    homes = jnp.stack([ma ^ t for t in range(ma_count)])
    wanted = jnp.where(reverse, ma_count - 1 - homes, homes).astype(jnp.int32)
    vmem = pl.BlockSpec(memory_space=pltpu.VMEM)
    smem = pl.BlockSpec(memory_space=pltpu.SMEM)
    params = pltpu.CompilerParams(vmem_limit_bytes=40 * 2**20)
    pieces = jnp.transpose(pod_modes, (3, 2, 1, 0, 4)).reshape(ma_count, 2, cells_x, fields, block, planes)
    piece = jax.ShapeDtypeStruct((2, cells_x, fields, block, planes), BF16)
    parts = pl.pallas_call(
        pack_kernel,
        out_shape=(piece,) * ma_count,
        in_specs=[smem, vmem],
        out_specs=(vmem,) * ma_count,
        compiler_params=params,
        cost_estimate=pl.CostEstimate(flops=0, bytes_accessed=2 * 2**20, transcendentals=0),
    )(wanted, pieces)
    parts = list(parts)
    for t in (2, 3, 1):
        parts[t] = lax.ppermute(parts[t], "ma", [(i, i ^ t) for i in range(ma_count)])

    def columns(part):
        return lax.dynamic_slice_in_dim(part, 2 * k, 2, 1).transpose(1, 0, 2).reshape(4, planes)

    vx, vy = columns(velocity[0]), columns(velocity[1])
    cells = jnp.stack([columns(velocity[2]), columns(region.astype(F32))])

    speeds = jnp.concatenate([vx, vy])
    place_of = jnp.stack([core, ma]).astype(jnp.int32)
    width = 4 * fields * planes
    wide = pltpu.VMEM((kinds, width), BF16)
    narrow = pltpu.VMEM((kinds, width // 2), BF16)

    def sums(terms):
        rows = (ma_count, terms * block, LANES)
        return jax.ShapeDtypeStruct(rows, F32), jax.ShapeDtypeStruct(rows, BF16)

    zc_keep, zc_send, modes = pl.pallas_call(
        local_kernel,
        out_shape=(*sums(2), jax.ShapeDtypeStruct((kinds, width), BF16)),
        in_specs=[smem, smem] + [vmem] * 6,
        out_specs=(vmem, vmem, vmem),
        scratch_shapes=[wide, wide],
        compiler_params=params,
        cost_estimate=pl.CostEstimate(flops=2 * 2 * kinds * kinds * width, bytes_accessed=4 * 2**20, transcendentals=0),
    )(place_of, coupling_table.reshape(-1, fields * fields), partner[None], cells, *parts)

    rows = jax.ShapeDtypeStruct((4 * fields * block + 16, LANES), BF16)
    first, second = pl.pallas_call(
        message_kernel,
        out_shape=(rows, rows),
        in_specs=[smem] + [vmem] * 5,
        out_specs=(vmem, vmem),
        compiler_params=params,
        cost_estimate=pl.CostEstimate(flops=0, bytes_accessed=2**20, transcendentals=0),
    )(place_of, speeds, *parts)

    def along_x(part, step):
        return lax.ppermute(part, ("gx", "ma"), steps_along_x(shape, step))

    def along_y(part, step):
        return lax.ppermute(part, names, steps_along_y(shape, step))

    xr, xl = along_x(second, -1), along_x(first, 1)
    yr, yl = along_y(first, -1), along_y(second, 1)

    keep, send = pl.pallas_call(
        edge_kernel,
        out_shape=sums(4),
        in_specs=[smem] + [vmem] * 8,
        out_specs=(vmem, vmem),
        scratch_shapes=[wide, narrow, narrow, wide, narrow, narrow],
        compiler_params=params,
        cost_estimate=pl.CostEstimate(flops=2 * 3 * kinds * kinds * width, bytes_accessed=6 * 2**20, transcendentals=0),
    )(place_of, speeds, modes, xr, xl, yr, yl, zc_keep, zc_send)

    def core_swap(part):
        return lax.ppermute(part, "core", [(i, 1 - i) for i in range(core_count)])

    shares = gx_count * y_count
    both = (keep + core_swap(send).astype(F32)).astype(BF16).reshape(ma_count * shares, -1, LANES)
    received = lax.all_to_all(both, ("ma", "gx", "y"), 0, 0)
    share = jnp.sum(received.astype(F32), axis=0) * scaling
    spread = jnp.broadcast_to(share[None], (shares * core_count,) + share.shape)
    whole = lax.all_to_all(spread, ("core", "gx", "y"), 0, 0)
    return whole.reshape(core_count, 4, block, LANES).transpose(1, 0, 3, 2).reshape(4, kinds, block)


def solution(mesh):
    gx, gy, ma = (mesh.shape[name] for name in ("gx", "gy", "ma"))
    split = Mesh(mesh.devices.reshape(gx, gy // 2, 2, ma), ("gx", "y", "core", "ma"))
    placed = (
        P("ma", None, "gx", ("y", "core"), None),
        P(None, "gx", ("y", "core"), None),
        P("gx", ("y", "core"), None),
        P(),
        P(),
    )
    return jax.shard_map(
        on_device, mesh=split, in_specs=placed, out_specs=P(None, None, "ma"), check_vma=False
    )
```

```python
import math

import jax
import jax.numpy as jnp
from jax import lax
from jax.experimental import pallas as pl
from jax.experimental.pallas import tpu as pltpu
from jax.sharding import Mesh, PartitionSpec as P

LANES = 128
BF16 = jnp.bfloat16
F32 = jnp.float32
CONTRACT_LAST = (((1,), (1,)), ((), ()))


def steps_along_x(shape, step):
    gx_count, y_count, core_count, ma_count = shape
    half = gx_count // 2
    pairs = []
    for gx in range(gx_count):
        to = gx + step
        if 0 <= to < gx_count:
            for ma in range(ma_count):
                to_ma = ma if gx // half == to // half else ma_count - 1 - ma
                pairs.append((gx * ma_count + ma, to * ma_count + to_ma))
    return pairs


def steps_along_y(shape, step):
    gx_count, y_count, core_count, ma_count = shape
    half = gx_count // 2
    gy_count = y_count * core_count

    def number(gx, place):
        gy, k = divmod(place, ma_count)
        ma = ma_count - 1 - k if (gx // half + gy) % 2 else k
        return (gx * gy_count + gy) * ma_count + ma

    places = gy_count * ma_count
    return [
        (number(gx, place), number(gx, place + step))
        for gx in range(gx_count)
        for place in range(places)
        if 0 <= place + step < places
    ]


def local_kernel(core, table, partner, cells, a, keep, send, modes, z_image, c_image):
    fields, block = a.shape[3], a.shape[4]
    planes = lax.broadcasted_iota(jnp.int32, (LANES, LANES), 0)
    pick = (planes == partner[...]).astype(F32).astype(BF16)
    speed_z, region = cells[0], cells[1]
    coupling = {}
    for f in range(fields):
        for g in range(fields):
            if f != g:
                chosen = jnp.zeros_like(region)
                for number in range(table.shape[0]):
                    chosen = jnp.where(region == float(number), table[number, f * fields + g], chosen)
                coupling[f, g] = chosen
    for col in range(4):
        for j in range(4):
            rows = slice(j * block, (j + 1) * block)
            here = [a[j, col // 2, col % 2, f] for f in range(fields)]
            moved = jnp.dot(jnp.concatenate(here, axis=0), pick, preferred_element_type=F32)
            centre = [cells_f.astype(F32) for cells_f in here]
            for f in range(fields):
                chunk = slice((col * fields + f) * LANES, (col * fields + f + 1) * LANES)
                modes[rows, chunk] = here[f]
                jump = speed_z[col : col + 1] * (moved[f * block : (f + 1) * block] - centre[f])
                z_image[rows, chunk] = jump.astype(BF16)
                running = None
                for g in range(fields):
                    if g != f:
                        term = coupling[f, g][col : col + 1] * centre[g]
                        running = term if running is None else running + term
                c_image[rows, chunk] = running.astype(BF16)
    for q, image in enumerate((z_image, c_image)):
        total = lax.dot_general(image[...], modes[...], CONTRACT_LAST, preferred_element_type=F32)
        place(core, keep, send, q, total, block)


def place(core, keep, send, q, total, block):
    for j in range(4):
        first = total[j * block : (j + 1) * block, :LANES]
        second = total[j * block : (j + 1) * block, LANES:]
        rows = slice(q * block, (q + 1) * block)
        keep[j, rows, :] = jnp.where(core[0] == 0, first, second)
        send[j, rows, :] = jnp.where(core[0] == 0, second, first).astype(BF16)


def edge_kernel(core, speeds, modes, xr, xl, yr, yl, zc_keep, zc_send, keep, send, x_image, x_edge, x_side, y_image, y_edge, y_side):
    fields, block = 4, modes.shape[0] // 4
    body = 4 * fields * block
    half_speeds = 0.5 * speeds[...]

    def beside_speed(message, axis):
        rows = message[body:, :].astype(F32)[3 * axis : 3 * axis + 3]
        return 0.5 * (rows[0:1] + rows[1:2] + rows[2:3])

    def lane_chunk(index):
        return slice(index * LANES, (index + 1) * LANES)

    axes = (
        (0, xr, xl, x_image, x_edge, x_side, lambda line, end: 2 * line + end),
        (4, yr, yl, y_image, y_edge, y_side, lambda line, end: 2 * end + line),
    )
    for axis, (base, after, before, image, edge, side, col) in enumerate(axes):
        for line, message in enumerate((before, after)):
            near_speed = half_speeds[base + col(line, 0) : base + col(line, 0) + 1]
            far_speed = half_speeds[base + col(line, 1) : base + col(line, 1) + 1]
            their_speed = beside_speed(message, axis)
            for j in range(4):
                rows = slice(j * block, (j + 1) * block)
                for f in range(fields):
                    near, far = (lane_chunk(col(line, end) * fields + f) for end in range(2))
                    extra = lane_chunk(line * fields + f)
                    m0 = modes[rows, near].astype(F32)
                    m1 = modes[rows, far].astype(F32)
                    start = (j * fields + f) * block
                    beside = message[start : start + block, :]
                    at_near = near_speed * m1
                    at_far = -far_speed * m0
                    if line == 1:
                        at_far = far_speed * beside.astype(F32) + at_far
                        at_side = -their_speed * m1
                    else:
                        at_near = at_near - near_speed * beside.astype(F32)
                        at_side = their_speed * m0
                    image[rows, near] = at_near.astype(BF16)
                    image[rows, far] = at_far.astype(BF16)
                    edge[rows, extra] = at_side.astype(BF16)
                    side[rows, extra] = beside
    for q, (_, _, _, image, edge, side, _) in enumerate(axes):
        total = lax.dot_general(image[...], modes[...], CONTRACT_LAST, preferred_element_type=F32)
        total += lax.dot_general(edge[...], side[...], CONTRACT_LAST, preferred_element_type=F32)
        place(core, keep, send, q, total, block)
    keep[:, 2 * block :, :] = zc_keep[...]
    send[:, 2 * block :, :] = zc_send[...]


def message_kernel(speeds, a, *messages):
    fields, block = a.shape[3], a.shape[4]
    body = 4 * fields * block
    for number, message in enumerate(messages):
        for j in range(4):
            for f in range(fields):
                start = (j * fields + f) * block
                message[start : start + block, :] = a[j, number, 1 - number, f]
        rows = []
        for axis in range(2):
            rest = speeds[4 * axis + 1 + number : 4 * axis + 2 + number, :]
            for _ in range(3):
                rows.append(rest.astype(BF16).astype(F32))
                rest = rest - rows[-1]
        rows.append(jnp.zeros((10, LANES), F32))
        message[body:, :] = jnp.concatenate(rows).astype(BF16)


def on_device(pod_modes, velocity, region, partner, coupling_table):
    block, fields, cells_x, cells_y, planes = pod_modes.shape
    names = ("gx", "y", "core", "ma")
    shape = tuple(lax.axis_size(name) for name in names)
    gx_count, y_count, core_count, ma_count = shape
    gx, y, core, ma = (lax.axis_index(name) for name in names)
    gy_count, gy = y_count * core_count, y * core_count + core
    cell_total = fields * cells_x * gx_count * cells_y * gy_count * planes
    scaling = 1.0 / math.sqrt(cell_total)
    kinds = block * ma_count
    reverse = (gx // (gx_count // 2) + gy) % 2 == 1
    k = jnp.where(reverse, ma_count - 1 - ma, ma)

    vmem = pl.BlockSpec(memory_space=pltpu.VMEM)
    smem = pl.BlockSpec(memory_space=pltpu.SMEM)
    params = pltpu.CompilerParams(vmem_limit_bytes=40 * 2**20)
    pieces = jnp.transpose(pod_modes, (3, 2, 1, 0, 4)).reshape(ma_count, 2, cells_x, fields, block, planes)
    a = lax.all_to_all(jnp.where(reverse, pieces[::-1], pieces), "ma", 0, 0)

    def columns(part):
        return lax.dynamic_slice_in_dim(part, 2 * k, 2, 1).transpose(1, 0, 2).reshape(4, planes)

    vx, vy = columns(velocity[0]), columns(velocity[1])
    cells = jnp.stack([columns(velocity[2]), columns(region.astype(F32))])

    speeds = jnp.concatenate([vx, vy])
    core_here = core.astype(jnp.int32)[None]
    width = 4 * fields * planes
    wide = pltpu.VMEM((kinds, width), BF16)
    narrow = pltpu.VMEM((kinds, width // 2), BF16)

    def sums(terms):
        rows = (ma_count, terms * block, LANES)
        return jax.ShapeDtypeStruct(rows, F32), jax.ShapeDtypeStruct(rows, BF16)

    zc_keep, zc_send, modes = pl.pallas_call(
        local_kernel,
        out_shape=(*sums(2), jax.ShapeDtypeStruct((kinds, width), BF16)),
        in_specs=[smem, smem] + [vmem] * 3,
        out_specs=(vmem, vmem, vmem),
        scratch_shapes=[wide, wide],
        compiler_params=params,
        cost_estimate=pl.CostEstimate(flops=2 * 2 * kinds * kinds * width, bytes_accessed=4 * 2**20, transcendentals=0),
    )(core_here, coupling_table.reshape(-1, fields * fields), partner[None], cells, a)

    rows = jax.ShapeDtypeStruct((4 * fields * block + 16, LANES), BF16)
    first, second = pl.pallas_call(
        message_kernel,
        out_shape=(rows, rows),
        in_specs=[vmem] * 2,
        out_specs=(vmem, vmem),
        compiler_params=params,
        cost_estimate=pl.CostEstimate(flops=0, bytes_accessed=2**20, transcendentals=0),
    )(speeds, a)

    def along_x(part, step):
        return lax.ppermute(part, ("gx", "ma"), steps_along_x(shape, step))

    def along_y(part, step):
        return lax.ppermute(part, names, steps_along_y(shape, step))

    yr, yl = along_y(first, -1), along_y(second, 1)
    xr, xl = along_x(second, -1), along_x(first, 1)

    keep, send = pl.pallas_call(
        edge_kernel,
        out_shape=sums(4),
        in_specs=[smem] + [vmem] * 8,
        out_specs=(vmem, vmem),
        scratch_shapes=[wide, narrow, narrow, wide, narrow, narrow],
        compiler_params=params,
        cost_estimate=pl.CostEstimate(flops=2 * 3 * kinds * kinds * width, bytes_accessed=6 * 2**20, transcendentals=0),
    )(core_here, speeds, modes, xr, xl, yr, yl, zc_keep, zc_send)

    def core_swap(part):
        return lax.ppermute(part, "core", [(i, 1 - i) for i in range(core_count)])

    shares = gx_count * y_count
    both = (keep + core_swap(send).astype(F32)).astype(BF16).reshape(ma_count * shares, -1, LANES)
    received = lax.all_to_all(both, ("ma", "gx", "y"), 0, 0)
    share = jnp.sum(received.astype(F32), axis=0) * scaling
    spread = jnp.broadcast_to(share[None], (shares * core_count,) + share.shape)
    whole = lax.all_to_all(spread, ("core", "gx", "y"), 0, 0)
    return whole.reshape(core_count, 4, block, LANES).transpose(1, 0, 3, 2).reshape(4, kinds, block)


def solution(mesh):
    gx, gy, ma = (mesh.shape[name] for name in ("gx", "gy", "ma"))
    split = Mesh(mesh.devices.reshape(gx, gy // 2, 2, ma), ("gx", "y", "core", "ma"))
    placed = (
        P("ma", None, "gx", ("y", "core"), None),
        P(None, "gx", ("y", "core"), None),
        P("gx", ("y", "core"), None),
        P(),
        P(),
    )
    return jax.shard_map(
        on_device, mesh=split, in_specs=placed, out_specs=P(None, None, "ma"), check_vma=False
    )
```

```python
import math

import jax
import jax.numpy as jnp
from jax import lax
from jax.experimental import pallas as pl
from jax.experimental.pallas import tpu as pltpu
from jax.sharding import Mesh, PartitionSpec as P

LANES = 128
BF16 = jnp.bfloat16
F32 = jnp.float32
CONTRACT_LAST = (((1,), (1,)), ((), ()))


def steps_along_x(shape, step):
    gx_count, y_count, core_count, ma_count = shape
    half = gx_count // 2
    pairs = []
    for gx in range(gx_count):
        to = gx + step
        if 0 <= to < gx_count:
            for ma in range(ma_count):
                to_ma = ma if gx // half == to // half else ma_count - 1 - ma
                pairs.append((gx * ma_count + ma, to * ma_count + to_ma))
    return pairs


def steps_along_y(shape, step):
    gx_count, y_count, core_count, ma_count = shape
    half = gx_count // 2
    gy_count = y_count * core_count

    def number(gx, place):
        gy, k = divmod(place, ma_count)
        ma = ma_count - 1 - k if (gx // half + gy) % 2 else k
        return (gx * gy_count + gy) * ma_count + ma

    places = gy_count * ma_count
    return [
        (number(gx, place), number(gx, place + step))
        for gx in range(gx_count)
        for place in range(places)
        if 0 <= place + step < places
    ]


def pack_kernel(wanted, pieces, *outs):
    for t in range(4):
        for number, (row, xi) in enumerate(((0, 1), (1, 0))):
            outs[t][number] = pieces[wanted[t], row, xi]
            outs[4 + t][number] = pieces[wanted[t], row, 1 - xi]


def local_kernel(place_of, table, partner, cells, *refs):
    early, late, (keep, send, modes, z_image, c_image) = refs[:4], refs[4:8], refs[8:]
    fields, block = early[0].shape[1], early[0].shape[2]
    planes = lax.broadcasted_iota(jnp.int32, (LANES, LANES), 0)
    pick = (planes == partner[...]).astype(F32).astype(BF16)
    speed_z, region = cells[0], cells[1]
    coupling = {}
    for f in range(fields):
        for g in range(fields):
            if f != g:
                chosen = jnp.zeros_like(region)
                for number in range(table.shape[0]):
                    chosen = jnp.where(region == float(number), table[number, f * fields + g], chosen)
                coupling[f, g] = chosen
    for col in range(4):
        for t in range(4):
            rows = pl.ds(pl.multiple_of((place_of[1] ^ t) * block, block), block)
            cell = (early if col in (1, 2) else late)[t]
            here = [cell[col // 2, f] for f in range(fields)]
            moved = jnp.dot(jnp.concatenate(here, axis=0), pick, preferred_element_type=F32)
            centre = [cells_f.astype(F32) for cells_f in here]
            for f in range(fields):
                chunk = slice((col * fields + f) * LANES, (col * fields + f + 1) * LANES)
                modes[rows, chunk] = here[f]
                jump = speed_z[col : col + 1] * (moved[f * block : (f + 1) * block] - centre[f])
                z_image[rows, chunk] = jump.astype(BF16)
                running = None
                for g in range(fields):
                    if g != f:
                        term = coupling[f, g][col : col + 1] * centre[g]
                        running = term if running is None else running + term
                c_image[rows, chunk] = running.astype(BF16)
    for q, image in enumerate((z_image, c_image)):
        total = lax.dot_general(image[...], modes[...], CONTRACT_LAST, preferred_element_type=F32)
        place(place_of, keep, send, q, total, block)


def place(place_of, keep, send, q, total, block):
    for j in range(4):
        first = total[j * block : (j + 1) * block, :LANES]
        second = total[j * block : (j + 1) * block, LANES:]
        rows = slice(q * block, (q + 1) * block)
        keep[j, rows, :] = jnp.where(place_of[0] == 0, first, second)
        send[j, rows, :] = jnp.where(place_of[0] == 0, second, first).astype(BF16)


def edge_kernel(place_of, speeds, modes, xr, xl, yr, yl, zc_keep, zc_send, keep, send, x_image, x_edge, x_side, y_image, y_edge, y_side):
    fields, block = 4, modes.shape[0] // 4
    body = 4 * fields * block
    half_speeds = 0.5 * speeds[...]

    def beside_speed(message, axis):
        rows = message[body:, :].astype(F32)[3 * axis : 3 * axis + 3]
        return 0.5 * (rows[0:1] + rows[1:2] + rows[2:3])

    def lane_chunk(index):
        return slice(index * LANES, (index + 1) * LANES)

    axes = (
        (0, xr, xl, x_image, x_edge, x_side, lambda line, end: 2 * line + end),
        (4, yr, yl, y_image, y_edge, y_side, lambda line, end: 2 * end + line),
    )
    for axis, (base, after, before, image, edge, side, col) in enumerate(axes):
        for line, message in enumerate((before, after)):
            near_speed = half_speeds[base + col(line, 0) : base + col(line, 0) + 1]
            far_speed = half_speeds[base + col(line, 1) : base + col(line, 1) + 1]
            their_speed = beside_speed(message, axis)
            for j in range(4):
                rows = slice(j * block, (j + 1) * block)
                for f in range(fields):
                    near, far = (lane_chunk(col(line, end) * fields + f) for end in range(2))
                    extra = lane_chunk(line * fields + f)
                    m0 = modes[rows, near].astype(F32)
                    m1 = modes[rows, far].astype(F32)
                    start = (j * fields + f) * block
                    beside = message[start : start + block, :]
                    at_near = near_speed * m1
                    at_far = -far_speed * m0
                    if line == 1:
                        at_far = far_speed * beside.astype(F32) + at_far
                        at_side = -their_speed * m1
                    else:
                        at_near = at_near - near_speed * beside.astype(F32)
                        at_side = their_speed * m0
                    image[rows, near] = at_near.astype(BF16)
                    image[rows, far] = at_far.astype(BF16)
                    edge[rows, extra] = at_side.astype(BF16)
                    side[rows, extra] = beside
    for q, (_, _, _, image, edge, side, _) in enumerate(axes):
        total = lax.dot_general(image[...], modes[...], CONTRACT_LAST, preferred_element_type=F32)
        total += lax.dot_general(edge[...], side[...], CONTRACT_LAST, preferred_element_type=F32)
        place(place_of, keep, send, q, total, block)
    keep[:, 2 * block :, :] = zc_keep[...]
    send[:, 2 * block :, :] = zc_send[...]


def message_kernel(place_of, speeds, *refs):
    parts, messages = refs[:4], refs[4:]
    fields, block = parts[0].shape[1], parts[0].shape[2]
    body = 4 * fields * block
    for number, message in enumerate(messages):
        for t in range(4):
            for f in range(fields):
                start = ((place_of[1] ^ t) * fields + f) * block
                message[pl.ds(pl.multiple_of(start, block), block), :] = parts[t][number, f]
        rows = []
        for axis in range(2):
            rest = speeds[4 * axis + 1 + number : 4 * axis + 2 + number, :]
            for _ in range(3):
                rows.append(rest.astype(BF16).astype(F32))
                rest = rest - rows[-1]
        rows.append(jnp.zeros((10, LANES), F32))
        message[body:, :] = jnp.concatenate(rows).astype(BF16)


def on_device(pod_modes, velocity, region, partner, coupling_table):
    block, fields, cells_x, cells_y, planes = pod_modes.shape
    names = ("gx", "y", "core", "ma")
    shape = tuple(lax.axis_size(name) for name in names)
    gx_count, y_count, core_count, ma_count = shape
    gx, y, core, ma = (lax.axis_index(name) for name in names)
    gy_count, gy = y_count * core_count, y * core_count + core
    cell_total = fields * cells_x * gx_count * cells_y * gy_count * planes
    scaling = 1.0 / math.sqrt(cell_total)
    kinds = block * ma_count
    reverse = (gx // (gx_count // 2) + gy) % 2 == 1
    k = jnp.where(reverse, ma_count - 1 - ma, ma)

    homes = jnp.stack([ma ^ t for t in range(ma_count)])
    wanted = jnp.where(reverse, ma_count - 1 - homes, homes).astype(jnp.int32)
    vmem = pl.BlockSpec(memory_space=pltpu.VMEM)
    smem = pl.BlockSpec(memory_space=pltpu.SMEM)
    params = pltpu.CompilerParams(vmem_limit_bytes=40 * 2**20)
    pieces = jnp.transpose(pod_modes, (3, 2, 1, 0, 4)).reshape(ma_count, 2, cells_x, fields, block, planes)
    piece = jax.ShapeDtypeStruct((2, fields, block, planes), BF16)
    packed = pl.pallas_call(
        pack_kernel,
        out_shape=(piece,) * (2 * ma_count),
        in_specs=[smem, vmem],
        out_specs=(vmem,) * (2 * ma_count),
        compiler_params=params,
        cost_estimate=pl.CostEstimate(flops=0, bytes_accessed=2 * 2**20, transcendentals=0),
    )(wanted, pieces)

    def collected(parts):
        blocks = {0: parts[0]}
        for t in (2, 3, 1):
            blocks[t] = lax.ppermute(parts[t], "ma", [(i, i ^ t) for i in range(ma_count)])
        return [blocks[t] for t in range(ma_count)]

    early, late = collected(packed[:ma_count]), collected(packed[ma_count:])

    def columns(part):
        return lax.dynamic_slice_in_dim(part, 2 * k, 2, 1).transpose(1, 0, 2).reshape(4, planes)

    vx, vy = columns(velocity[0]), columns(velocity[1])
    cells = jnp.stack([columns(velocity[2]), columns(region.astype(F32))])

    speeds = jnp.concatenate([vx, vy])
    place_of = jnp.stack([core, ma]).astype(jnp.int32)
    width = 4 * fields * planes
    wide = pltpu.VMEM((kinds, width), BF16)
    narrow = pltpu.VMEM((kinds, width // 2), BF16)

    def sums(terms):
        rows = (ma_count, terms * block, LANES)
        return jax.ShapeDtypeStruct(rows, F32), jax.ShapeDtypeStruct(rows, BF16)

    zc_keep, zc_send, modes = pl.pallas_call(
        local_kernel,
        out_shape=(*sums(2), jax.ShapeDtypeStruct((kinds, width), BF16)),
        in_specs=[smem, smem] + [vmem] * 10,
        out_specs=(vmem, vmem, vmem),
        scratch_shapes=[wide, wide],
        compiler_params=params,
        cost_estimate=pl.CostEstimate(flops=2 * 2 * kinds * kinds * width, bytes_accessed=4 * 2**20, transcendentals=0),
    )(place_of, coupling_table.reshape(-1, fields * fields), partner[None], cells, *early, *late)

    rows = jax.ShapeDtypeStruct((4 * fields * block + 16, LANES), BF16)
    first, second = pl.pallas_call(
        message_kernel,
        out_shape=(rows, rows),
        in_specs=[smem] + [vmem] * 5,
        out_specs=(vmem, vmem),
        compiler_params=params,
        cost_estimate=pl.CostEstimate(flops=0, bytes_accessed=2**20, transcendentals=0),
    )(place_of, speeds, *early)

    def along_x(part, step):
        return lax.ppermute(part, ("gx", "ma"), steps_along_x(shape, step))

    def along_y(part, step):
        return lax.ppermute(part, names, steps_along_y(shape, step))

    xr, xl = along_x(second, -1), along_x(first, 1)
    yr, yl = along_y(first, -1), along_y(second, 1)

    keep, send = pl.pallas_call(
        edge_kernel,
        out_shape=sums(4),
        in_specs=[smem] + [vmem] * 8,
        out_specs=(vmem, vmem),
        scratch_shapes=[wide, narrow, narrow, wide, narrow, narrow],
        compiler_params=params,
        cost_estimate=pl.CostEstimate(flops=2 * 3 * kinds * kinds * width, bytes_accessed=6 * 2**20, transcendentals=0),
    )(place_of, speeds, modes, xr, xl, yr, yl, zc_keep, zc_send)

    def core_swap(part):
        return lax.ppermute(part, "core", [(i, 1 - i) for i in range(core_count)])

    shares = gx_count * y_count
    both = (keep + core_swap(send).astype(F32)).astype(BF16).reshape(ma_count * shares, -1, LANES)
    received = lax.all_to_all(both, ("ma", "gx", "y"), 0, 0)
    share = jnp.sum(received.astype(F32), axis=0) * scaling
    spread = jnp.broadcast_to(share[None], (shares * core_count,) + share.shape)
    whole = lax.all_to_all(spread, ("core", "gx", "y"), 0, 0)
    return whole.reshape(core_count, 4, block, LANES).transpose(1, 0, 3, 2).reshape(4, kinds, block)


def solution(mesh):
    gx, gy, ma = (mesh.shape[name] for name in ("gx", "gy", "ma"))
    split = Mesh(mesh.devices.reshape(gx, gy // 2, 2, ma), ("gx", "y", "core", "ma"))
    placed = (
        P("ma", None, "gx", ("y", "core"), None),
        P(None, "gx", ("y", "core"), None),
        P("gx", ("y", "core"), None),
        P(),
        P(),
    )
    return jax.shard_map(
        on_device, mesh=split, in_specs=placed, out_specs=P(None, None, "ma"), check_vma=False
    )
```

```python
import math

import jax
import jax.numpy as jnp
from jax import lax
from jax.experimental import pallas as pl
from jax.experimental.pallas import tpu as pltpu
from jax.sharding import Mesh, PartitionSpec as P

LANES = 128
BF16 = jnp.bfloat16
F32 = jnp.float32
CONTRACT_LAST = (((1,), (1,)), ((), ()))


def steps_along_x(shape, step):
    gx_count, y_count, core_count, ma_count = shape
    half = gx_count // 2
    pairs = []
    for gx in range(gx_count):
        to = gx + step
        if 0 <= to < gx_count:
            for ma in range(ma_count):
                to_ma = ma if gx // half == to // half else ma_count - 1 - ma
                pairs.append((gx * ma_count + ma, to * ma_count + to_ma))
    return pairs


def steps_along_y(shape, step):
    gx_count, y_count, core_count, ma_count = shape
    half = gx_count // 2
    gy_count = y_count * core_count

    def number(gx, place):
        gy, k = divmod(place, ma_count)
        ma = ma_count - 1 - k if (gx // half + gy) % 2 else k
        return (gx * gy_count + gy) * ma_count + ma

    places = gy_count * ma_count
    return [
        (number(gx, place), number(gx, place + step))
        for gx in range(gx_count)
        for place in range(places)
        if 0 <= place + step < places
    ]


def pack_kernel(wanted, pieces, *outs):
    for t in range(4):
        for number, (row, xi) in enumerate(((0, 1), (1, 0))):
            outs[t][number] = pieces[wanted[t], row, xi]
            outs[4 + t][number] = pieces[wanted[t], row, 1 - xi]


def local_kernel(place_of, table, cells, *refs):
    early, late, (keep, send, modes, z_image, c_image) = refs[:4], refs[4:8], refs[8:]
    fields, block = early[0].shape[1], early[0].shape[2]
    planes = lax.broadcasted_iota(jnp.int32, (LANES, LANES), 0).astype(F32)
    speed_z, region, partner = cells[:4, :], cells[4:8, :], cells[8:9, :]
    pick = (planes == partner).astype(F32).astype(BF16)
    coupling = {}
    for f in range(fields):
        for g in range(fields):
            if f != g:
                chosen = jnp.zeros_like(region)
                for number in range(table.shape[0]):
                    chosen = jnp.where(region == float(number), table[number, f * fields + g], chosen)
                coupling[f, g] = chosen
    for col in range(4):
        for t in range(4):
            rows = pl.ds(pl.multiple_of((place_of[1] ^ t) * block, block), block)
            cell = (early if col in (1, 2) else late)[t]
            here = [cell[col // 2, f] for f in range(fields)]
            moved = jnp.dot(jnp.concatenate(here, axis=0), pick, preferred_element_type=F32)
            centre = [cells_f.astype(F32) for cells_f in here]
            for f in range(fields):
                chunk = slice((col * fields + f) * LANES, (col * fields + f + 1) * LANES)
                modes[rows, chunk] = here[f]
                jump = speed_z[col : col + 1] * (moved[f * block : (f + 1) * block] - centre[f])
                z_image[rows, chunk] = jump.astype(BF16)
                running = None
                for g in range(fields):
                    if g != f:
                        term = coupling[f, g][col : col + 1] * centre[g]
                        running = term if running is None else running + term
                c_image[rows, chunk] = running.astype(BF16)
    for q, image in enumerate((z_image, c_image)):
        total = lax.dot_general(image[...], modes[...], CONTRACT_LAST, preferred_element_type=F32)
        place(place_of, keep, send, q, total, block)


def place(place_of, keep, send, q, total, block):
    for j in range(4):
        first = total[j * block : (j + 1) * block, :LANES]
        second = total[j * block : (j + 1) * block, LANES:]
        rows = slice(q * block, (q + 1) * block)
        keep[j, rows, :] = jnp.where(place_of[0] == 0, first, second)
        send[j, rows, :] = jnp.where(place_of[0] == 0, second, first).astype(BF16)


def edge_kernel(place_of, speeds, modes, xr, xl, yr, yl, zc_keep, zc_send, keep, send, x_image, x_edge, x_side, y_image, y_edge, y_side):
    fields, block = 4, modes.shape[0] // 4
    body = 4 * fields * block
    half_speeds = 0.5 * speeds[...]

    def beside_speed(message, axis):
        rows = message[body:, :].astype(F32)[3 * axis : 3 * axis + 3]
        return 0.5 * (rows[0:1] + rows[1:2] + rows[2:3])

    def lane_chunk(index):
        return slice(index * LANES, (index + 1) * LANES)

    axes = (
        (0, xr, xl, x_image, x_edge, x_side, lambda line, end: 2 * line + end),
        (4, yr, yl, y_image, y_edge, y_side, lambda line, end: 2 * end + line),
    )
    for axis, (base, after, before, image, edge, side, col) in enumerate(axes):
        for line, message in enumerate((before, after)):
            near_speed = half_speeds[base + col(line, 0) : base + col(line, 0) + 1]
            far_speed = half_speeds[base + col(line, 1) : base + col(line, 1) + 1]
            their_speed = beside_speed(message, axis)
            for j in range(4):
                rows = slice(j * block, (j + 1) * block)
                for f in range(fields):
                    near, far = (lane_chunk(col(line, end) * fields + f) for end in range(2))
                    extra = lane_chunk(line * fields + f)
                    m0 = modes[rows, near].astype(F32)
                    m1 = modes[rows, far].astype(F32)
                    start = (j * fields + f) * block
                    beside = message[start : start + block, :]
                    at_near = near_speed * m1
                    at_far = -far_speed * m0
                    if line == 1:
                        at_far = far_speed * beside.astype(F32) + at_far
                        at_side = -their_speed * m1
                    else:
                        at_near = at_near - near_speed * beside.astype(F32)
                        at_side = their_speed * m0
                    image[rows, near] = at_near.astype(BF16)
                    image[rows, far] = at_far.astype(BF16)
                    edge[rows, extra] = at_side.astype(BF16)
                    side[rows, extra] = beside
    for q, (_, _, _, image, edge, side, _) in enumerate(axes):
        total = lax.dot_general(image[...], modes[...], CONTRACT_LAST, preferred_element_type=F32)
        total += lax.dot_general(edge[...], side[...], CONTRACT_LAST, preferred_element_type=F32)
        place(place_of, keep, send, q, total, block)
    keep[:, 2 * block :, :] = zc_keep[...]
    send[:, 2 * block :, :] = zc_send[...]


def message_kernel(place_of, speeds, cells, *refs):
    parts, messages = refs[:4], refs[4:]
    fields, block = parts[0].shape[1], parts[0].shape[2]
    body = 4 * fields * block
    for number, message in enumerate(messages):
        for t in range(4):
            for f in range(fields):
                start = ((place_of[1] ^ t) * fields + f) * block
                message[pl.ds(pl.multiple_of(start, block), block), :] = parts[t][number, f]
        rows = []
        for axis in range(2):
            rest = speeds[4 * axis + 1 + number : 4 * axis + 2 + number, :]
            for _ in range(3):
                rows.append(rest.astype(BF16).astype(F32))
                rest = rest - rows[-1]
        rows.append(jnp.zeros((10, LANES), F32))
        message[body:, :] = jnp.concatenate(rows).astype(BF16)


def on_device(pod_modes, velocity, region, partner, coupling_table):
    block, fields, cells_x, cells_y, planes = pod_modes.shape
    names = ("gx", "y", "core", "ma")
    shape = tuple(lax.axis_size(name) for name in names)
    gx_count, y_count, core_count, ma_count = shape
    gx, y, core, ma = (lax.axis_index(name) for name in names)
    gy_count, gy = y_count * core_count, y * core_count + core
    cell_total = fields * cells_x * gx_count * cells_y * gy_count * planes
    scaling = 1.0 / math.sqrt(cell_total)
    kinds = block * ma_count
    reverse = (gx // (gx_count // 2) + gy) % 2 == 1
    k = jnp.where(reverse, ma_count - 1 - ma, ma)

    homes = jnp.stack([ma ^ t for t in range(ma_count)])
    wanted = jnp.where(reverse, ma_count - 1 - homes, homes).astype(jnp.int32)
    vmem = pl.BlockSpec(memory_space=pltpu.VMEM)
    smem = pl.BlockSpec(memory_space=pltpu.SMEM)
    params = pltpu.CompilerParams(vmem_limit_bytes=40 * 2**20)
    pieces = jnp.transpose(pod_modes, (3, 2, 1, 0, 4)).reshape(ma_count, 2, cells_x, fields, block, planes)
    piece = jax.ShapeDtypeStruct((2, fields, block, planes), BF16)
    packed = pl.pallas_call(
        pack_kernel,
        out_shape=(piece,) * (2 * ma_count),
        in_specs=[smem, vmem],
        out_specs=(vmem,) * (2 * ma_count),
        compiler_params=params,
        cost_estimate=pl.CostEstimate(flops=0, bytes_accessed=2 * 2**20, transcendentals=0),
    )(wanted, pieces)

    def collected(parts):
        blocks = {0: parts[0]}
        for t in (2, 3, 1):
            blocks[t] = lax.ppermute(parts[t], "ma", [(i, i ^ t) for i in range(ma_count)])
        return [blocks[t] for t in range(ma_count)]

    early, late = collected(packed[:ma_count]), collected(packed[ma_count:])

    def columns(part):
        return lax.dynamic_slice_in_dim(part, 2 * k, 2, 1).transpose(1, 0, 2).reshape(4, planes)

    vx, vy = columns(velocity[0]), columns(velocity[1])
    partners = jnp.broadcast_to(partner.astype(F32)[None], (8, planes))
    cells = jnp.concatenate([columns(velocity[2]), columns(region.astype(F32)), partners])

    speeds = jnp.concatenate([vx, vy])
    place_of = jnp.stack([core, ma]).astype(jnp.int32)
    width = 4 * fields * planes
    wide = pltpu.VMEM((kinds, width), BF16)
    narrow = pltpu.VMEM((kinds, width // 2), BF16)

    def sums(terms):
        rows = (ma_count, terms * block, LANES)
        return jax.ShapeDtypeStruct(rows, F32), jax.ShapeDtypeStruct(rows, BF16)

    zc_keep, zc_send, modes = pl.pallas_call(
        local_kernel,
        out_shape=(*sums(2), jax.ShapeDtypeStruct((kinds, width), BF16)),
        in_specs=[smem, smem] + [vmem] * 9,
        out_specs=(vmem, vmem, vmem),
        scratch_shapes=[wide, wide],
        compiler_params=params,
        cost_estimate=pl.CostEstimate(flops=2 * 2 * kinds * kinds * width, bytes_accessed=4 * 2**20, transcendentals=0),
    )(place_of, coupling_table.reshape(-1, fields * fields), cells, *early, *late)

    rows = jax.ShapeDtypeStruct((4 * fields * block + 16, LANES), BF16)
    first, second = pl.pallas_call(
        message_kernel,
        out_shape=(rows, rows),
        in_specs=[smem] + [vmem] * 6,
        out_specs=(vmem, vmem),
        compiler_params=params,
        cost_estimate=pl.CostEstimate(flops=0, bytes_accessed=2**20, transcendentals=0),
    )(place_of, speeds, cells, *early)

    def along_x(part, step):
        return lax.ppermute(part, ("gx", "ma"), steps_along_x(shape, step))

    def along_y(part, step):
        return lax.ppermute(part, names, steps_along_y(shape, step))

    xr, xl = along_x(second, -1), along_x(first, 1)
    yr, yl = along_y(first, -1), along_y(second, 1)

    keep, send = pl.pallas_call(
        edge_kernel,
        out_shape=sums(4),
        in_specs=[smem] + [vmem] * 8,
        out_specs=(vmem, vmem),
        scratch_shapes=[wide, narrow, narrow, wide, narrow, narrow],
        compiler_params=params,
        cost_estimate=pl.CostEstimate(flops=2 * 3 * kinds * kinds * width, bytes_accessed=6 * 2**20, transcendentals=0),
    )(place_of, speeds, modes, xr, xl, yr, yl, zc_keep, zc_send)

    def core_swap(part):
        return lax.ppermute(part, "core", [(i, 1 - i) for i in range(core_count)])

    shares = gx_count * y_count
    both = (keep + core_swap(send).astype(F32)).astype(BF16).reshape(ma_count * shares, -1, LANES)
    received = lax.all_to_all(both, ("ma", "gx", "y"), 0, 0)
    share = jnp.sum(received.astype(F32), axis=0) * scaling
    spread = jnp.broadcast_to(share.astype(BF16)[None], (shares * core_count,) + share.shape)
    whole = lax.all_to_all(spread, ("core", "gx", "y"), 0, 0)
    return whole.reshape(core_count, 4, block, LANES).transpose(1, 0, 3, 2).reshape(4, kinds, block).astype(F32)


def solution(mesh):
    gx, gy, ma = (mesh.shape[name] for name in ("gx", "gy", "ma"))
    split = Mesh(mesh.devices.reshape(gx, gy // 2, 2, ma), ("gx", "y", "core", "ma"))
    placed = (
        P("ma", None, "gx", ("y", "core"), None),
        P(None, "gx", ("y", "core"), None),
        P("gx", ("y", "core"), None),
        P(),
        P(),
    )
    return jax.shard_map(
        on_device, mesh=split, in_specs=placed, out_specs=P(None, None, "ma"), check_vma=False
    )
```

```python
import math

import jax
import jax.numpy as jnp
from jax import lax
from jax.experimental import pallas as pl
from jax.experimental.pallas import tpu as pltpu
from jax.sharding import Mesh, PartitionSpec as P

LANES = 128
BF16 = jnp.bfloat16
F32 = jnp.float32
CONTRACT_LAST = (((1,), (1,)), ((), ()))


def steps_along_x(shape, step):
    gx_count, y_count, core_count, ma_count = shape
    half = gx_count // 2
    pairs = []
    for gx in range(gx_count):
        to = gx + step
        if 0 <= to < gx_count:
            for ma in range(ma_count):
                to_ma = ma if gx // half == to // half else ma_count - 1 - ma
                pairs.append((gx * ma_count + ma, to * ma_count + to_ma))
    return pairs


def steps_along_y(shape, step):
    gx_count, y_count, core_count, ma_count = shape
    half = gx_count // 2
    gy_count = y_count * core_count

    def number(gx, place):
        gy, k = divmod(place, ma_count)
        ma = ma_count - 1 - k if (gx // half + gy) % 2 else k
        return (gx * gy_count + gy) * ma_count + ma

    places = gy_count * ma_count
    return [
        (number(gx, place), number(gx, place + step))
        for gx in range(gx_count)
        for place in range(places)
        if 0 <= place + step < places
    ]


def pack_kernel(wanted, pieces, *outs):
    for t in range(4):
        for number, (row, xi) in enumerate(((0, 1), (1, 0))):
            outs[t][number] = pieces[wanted[t], row, xi]
            outs[4 + t][number] = pieces[wanted[t], row, 1 - xi]


def local_kernel(place_of, table, cells, *refs):
    early, late, (keep, send, modes, z_image, c_image) = refs[:4], refs[4:8], refs[8:]
    fields, block = early[0].shape[1], early[0].shape[2]
    planes = lax.broadcasted_iota(jnp.int32, (LANES, LANES), 0).astype(F32)
    speed_z, region, partner = cells[:4, :], cells[4:8, :], cells[8:9, :]
    pick = (planes == partner).astype(F32).astype(BF16)
    coupling = {}
    for f in range(fields):
        for g in range(fields):
            if f != g:
                chosen = jnp.zeros_like(region)
                for number in range(table.shape[0]):
                    chosen = jnp.where(region == float(number), table[number, f * fields + g], chosen)
                coupling[f, g] = chosen
    for col in range(4):
        for t in range(4):
            rows = pl.ds(pl.multiple_of((place_of[1] ^ t) * block, block), block)
            cell = (early if col in (1, 2) else late)[t]
            here = [cell[col // 2, f] for f in range(fields)]
            moved = jnp.dot(jnp.concatenate(here, axis=0), pick, preferred_element_type=F32)
            centre = [cells_f.astype(F32) for cells_f in here]
            for f in range(fields):
                chunk = slice((col * fields + f) * LANES, (col * fields + f + 1) * LANES)
                modes[rows, chunk] = here[f]
                jump = speed_z[col : col + 1] * (moved[f * block : (f + 1) * block] - centre[f])
                z_image[rows, chunk] = jump.astype(BF16)
                running = None
                for g in range(fields):
                    if g != f:
                        term = coupling[f, g][col : col + 1] * centre[g]
                        running = term if running is None else running + term
                c_image[rows, chunk] = running.astype(BF16)
    for q, image in enumerate((z_image, c_image)):
        total = lax.dot_general(image[...], modes[...], CONTRACT_LAST, preferred_element_type=F32)
        place(place_of, keep, send, q, total, block)


def place(place_of, keep, send, q, total, block):
    for j in range(4):
        first = total[j * block : (j + 1) * block, :LANES]
        second = total[j * block : (j + 1) * block, LANES:]
        rows = slice(q * block, (q + 1) * block)
        keep[j, rows, :] = jnp.where(place_of[0] == 0, first, second)
        send[j, rows, :] = jnp.where(place_of[0] == 0, second, first).astype(BF16)


def edge_kernel(place_of, speeds, modes, xr, xl, yr, yl, zc_keep, zc_send, keep, send, x_image, x_edge, x_side, y_image, y_edge, y_side):
    fields, block = 4, modes.shape[0] // 4
    body = 4 * fields * block
    half_speeds = 0.5 * speeds[...]

    def beside_speed(message, axis):
        rows = message[body:, :].astype(F32)[3 * axis : 3 * axis + 3]
        return 0.5 * (rows[0:1] + rows[1:2] + rows[2:3])

    def lane_chunk(index):
        return slice(index * LANES, (index + 1) * LANES)

    axes = (
        (0, xr, xl, x_image, x_edge, x_side, lambda line, end: 2 * line + end),
        (4, yr, yl, y_image, y_edge, y_side, lambda line, end: 2 * end + line),
    )
    for axis, (base, after, before, image, edge, side, col) in enumerate(axes):
        for line, message in enumerate((before, after)):
            near_speed = half_speeds[base + col(line, 0) : base + col(line, 0) + 1]
            far_speed = half_speeds[base + col(line, 1) : base + col(line, 1) + 1]
            their_speed = beside_speed(message, axis)
            for j in range(4):
                rows = slice(j * block, (j + 1) * block)
                for f in range(fields):
                    near, far = (lane_chunk(col(line, end) * fields + f) for end in range(2))
                    extra = lane_chunk(line * fields + f)
                    m0 = modes[rows, near].astype(F32)
                    m1 = modes[rows, far].astype(F32)
                    start = (j * fields + f) * block
                    beside = message[start : start + block, :]
                    at_near = near_speed * m1
                    at_far = -far_speed * m0
                    if line == 1:
                        at_far = far_speed * beside.astype(F32) + at_far
                        at_side = -their_speed * m1
                    else:
                        at_near = at_near - near_speed * beside.astype(F32)
                        at_side = their_speed * m0
                    image[rows, near] = at_near.astype(BF16)
                    image[rows, far] = at_far.astype(BF16)
                    edge[rows, extra] = at_side.astype(BF16)
                    side[rows, extra] = beside
    for q, (_, _, _, image, edge, side, _) in enumerate(axes):
        total = lax.dot_general(image[...], modes[...], CONTRACT_LAST, preferred_element_type=F32)
        total += lax.dot_general(edge[...], side[...], CONTRACT_LAST, preferred_element_type=F32)
        place(place_of, keep, send, q, total, block)
    keep[:, 2 * block :, :] = zc_keep[...]
    send[:, 2 * block :, :] = zc_send[...]


def message_kernel(place_of, speeds, *refs):
    parts, messages = refs[:4], refs[4:]
    fields, block = parts[0].shape[1], parts[0].shape[2]
    body = 4 * fields * block
    for number, message in enumerate(messages):
        for t in range(4):
            for f in range(fields):
                start = ((place_of[1] ^ t) * fields + f) * block
                message[pl.ds(pl.multiple_of(start, block), block), :] = parts[t][number, f]
        rows = []
        for axis in range(2):
            rest = speeds[4 * axis + 1 + number : 4 * axis + 2 + number, :]
            for _ in range(3):
                rows.append(rest.astype(BF16).astype(F32))
                rest = rest - rows[-1]
        rows.append(jnp.zeros((10, LANES), F32))
        message[body:, :] = jnp.concatenate(rows).astype(BF16)


def on_device(pod_modes, velocity, region, partner, coupling_table):
    block, fields, cells_x, cells_y, planes = pod_modes.shape
    names = ("gx", "y", "core", "ma")
    shape = tuple(lax.axis_size(name) for name in names)
    gx_count, y_count, core_count, ma_count = shape
    gx, y, core, ma = (lax.axis_index(name) for name in names)
    gy_count, gy = y_count * core_count, y * core_count + core
    cell_total = fields * cells_x * gx_count * cells_y * gy_count * planes
    scaling = 1.0 / math.sqrt(cell_total)
    kinds = block * ma_count
    reverse = (gx // (gx_count // 2) + gy) % 2 == 1
    k = jnp.where(reverse, ma_count - 1 - ma, ma)

    homes = jnp.stack([ma ^ t for t in range(ma_count)])
    wanted = jnp.where(reverse, ma_count - 1 - homes, homes).astype(jnp.int32)
    vmem = pl.BlockSpec(memory_space=pltpu.VMEM)
    smem = pl.BlockSpec(memory_space=pltpu.SMEM)
    params = pltpu.CompilerParams(vmem_limit_bytes=40 * 2**20)
    pieces = jnp.transpose(pod_modes, (3, 2, 1, 0, 4)).reshape(ma_count, 2, cells_x, fields, block, planes)
    piece = jax.ShapeDtypeStruct((2, fields, block, planes), BF16)
    packed = pl.pallas_call(
        pack_kernel,
        out_shape=(piece,) * (2 * ma_count),
        in_specs=[smem, vmem],
        out_specs=(vmem,) * (2 * ma_count),
        compiler_params=params,
        cost_estimate=pl.CostEstimate(flops=0, bytes_accessed=2 * 2**20, transcendentals=0),
    )(wanted, pieces)

    def collected(parts):
        blocks = {0: parts[0]}
        for t in (2, 3, 1):
            blocks[t] = lax.ppermute(parts[t], "ma", [(i, i ^ t) for i in range(ma_count)])
        return [blocks[t] for t in range(ma_count)]

    early, late = collected(packed[:ma_count]), collected(packed[ma_count:])

    def columns(part):
        return lax.dynamic_slice_in_dim(part, 2 * k, 2, 1).transpose(1, 0, 2).reshape(4, planes)

    vx, vy = columns(velocity[0]), columns(velocity[1])
    partners = jnp.broadcast_to(partner.astype(F32)[None], (8, planes))
    cells = jnp.concatenate([columns(velocity[2]), columns(region.astype(F32)), partners])

    speeds = jnp.concatenate([vx, vy])
    place_of = jnp.stack([core, ma]).astype(jnp.int32)
    width = 4 * fields * planes
    wide = pltpu.VMEM((kinds, width), BF16)
    narrow = pltpu.VMEM((kinds, width // 2), BF16)

    def sums(terms):
        rows = (ma_count, terms * block, LANES)
        return jax.ShapeDtypeStruct(rows, F32), jax.ShapeDtypeStruct(rows, BF16)

    zc_keep, zc_send, modes = pl.pallas_call(
        local_kernel,
        out_shape=(*sums(2), jax.ShapeDtypeStruct((kinds, width), BF16)),
        in_specs=[smem, smem] + [vmem] * 9,
        out_specs=(vmem, vmem, vmem),
        scratch_shapes=[wide, wide],
        compiler_params=params,
        cost_estimate=pl.CostEstimate(flops=2 * 2 * kinds * kinds * width, bytes_accessed=4 * 2**20, transcendentals=0),
    )(place_of, coupling_table.reshape(-1, fields * fields), cells, *early, *late)

    rows = jax.ShapeDtypeStruct((4 * fields * block + 16, LANES), BF16)
    first, second = pl.pallas_call(
        message_kernel,
        out_shape=(rows, rows),
        in_specs=[smem] + [vmem] * 5,
        out_specs=(vmem, vmem),
        compiler_params=params,
        cost_estimate=pl.CostEstimate(flops=0, bytes_accessed=2**20, transcendentals=0),
    )(place_of, speeds, *early)

    def along_x(part, step):
        return lax.ppermute(part, ("gx", "ma"), steps_along_x(shape, step))

    def along_y(part, step):
        return lax.ppermute(part, names, steps_along_y(shape, step))

    xr, xl = along_x(second, -1), along_x(first, 1)
    yr, yl = along_y(first, -1), along_y(second, 1)

    keep, send = pl.pallas_call(
        edge_kernel,
        out_shape=sums(4),
        in_specs=[smem] + [vmem] * 8,
        out_specs=(vmem, vmem),
        scratch_shapes=[wide, narrow, narrow, wide, narrow, narrow],
        compiler_params=params,
        cost_estimate=pl.CostEstimate(flops=2 * 3 * kinds * kinds * width, bytes_accessed=6 * 2**20, transcendentals=0),
    )(place_of, speeds, modes, xr, xl, yr, yl, zc_keep, zc_send)

    def core_swap(part):
        return lax.ppermute(part, "core", [(i, 1 - i) for i in range(core_count)])

    shares = gx_count * y_count
    both = (keep + core_swap(send).astype(F32)).astype(BF16).reshape(ma_count * shares, -1, LANES)
    received = lax.all_to_all(both, ("ma", "gx", "y"), 0, 0)
    share = jnp.sum(received.astype(F32), axis=0) * scaling
    spread = jnp.broadcast_to(share.astype(BF16)[None], (shares * core_count,) + share.shape)
    whole = lax.all_to_all(spread, ("core", "gx", "y"), 0, 0)
    return whole.reshape(core_count, 4, block, LANES).transpose(1, 0, 3, 2).reshape(4, kinds, block).astype(F32)


def solution(mesh):
    gx, gy, ma = (mesh.shape[name] for name in ("gx", "gy", "ma"))
    split = Mesh(mesh.devices.reshape(gx, gy // 2, 2, ma), ("gx", "y", "core", "ma"))
    placed = (
        P("ma", None, "gx", ("y", "core"), None),
        P(None, "gx", ("y", "core"), None),
        P("gx", ("y", "core"), None),
        P(),
        P(),
    )
    return jax.shard_map(
        on_device, mesh=split, in_specs=placed, out_specs=P(None, None, "ma"), check_vma=False
    )
```

```python
import math

import jax
import jax.numpy as jnp
from jax import lax
from jax.experimental import pallas as pl
from jax.experimental.pallas import tpu as pltpu
from jax.sharding import Mesh, PartitionSpec as P

LANES = 128
BF16 = jnp.bfloat16
F32 = jnp.float32
CONTRACT_LAST = (((1,), (1,)), ((), ()))


def steps_along_x(shape, step):
    gx_count, y_count, core_count, ma_count = shape
    half = gx_count // 2
    pairs = []
    for gx in range(gx_count):
        to = gx + step
        if 0 <= to < gx_count:
            for ma in range(ma_count):
                to_ma = ma if gx // half == to // half else ma_count - 1 - ma
                pairs.append((gx * ma_count + ma, to * ma_count + to_ma))
    return pairs


def steps_along_y(shape, step):
    gx_count, y_count, core_count, ma_count = shape
    half = gx_count // 2
    gy_count = y_count * core_count

    def number(gx, place):
        gy, k = divmod(place, ma_count)
        ma = ma_count - 1 - k if (gx // half + gy) % 2 else k
        return (gx * gy_count + gy) * ma_count + ma

    places = gy_count * ma_count
    return [
        (number(gx, place), number(gx, place + step))
        for gx in range(gx_count)
        for place in range(places)
        if 0 <= place + step < places
    ]


def pack_kernel(wanted, pieces, *outs):
    for t in range(4):
        for number, (row, xi) in enumerate(((0, 1), (1, 0))):
            outs[t][number] = pieces[wanted[t], row, xi]
            outs[4 + t][number] = pieces[wanted[t], row, 1 - xi]


def write_messages(axis, place_of, speeds, parts, messages):
    fields, block = parts[0].shape[1], parts[0].shape[2]
    body = 4 * fields * block
    for number, message in enumerate(messages):
        for t in range(4):
            for f in range(fields):
                start = ((place_of[1] ^ t) * fields + f) * block
                message[pl.ds(pl.multiple_of(start, block), block), :] = parts[t][number, f]
        rows = []
        rest = speeds[4 * axis + 1 + number : 4 * axis + 2 + number, :]
        for _ in range(3):
            rows.append(rest.astype(BF16).astype(F32))
            rest = rest - rows[-1]
        rows.append(jnp.zeros((13, LANES), F32))
        message[body:, :] = jnp.concatenate(rows).astype(BF16)


def message_kernel(place_of, speeds, *refs):
    write_messages(0, place_of, speeds, refs[:4], refs[4:])


def local_kernel(place_of, table, cells, speeds, *refs):
    early, late, (keep, send, modes, first, second, z_image, c_image) = refs[:4], refs[4:8], refs[8:]
    write_messages(1, place_of, speeds, early, (first, second))
    fields, block = early[0].shape[1], early[0].shape[2]
    planes = lax.broadcasted_iota(jnp.int32, (LANES, LANES), 0).astype(F32)
    speed_z, region, partner = cells[:4, :], cells[4:8, :], cells[8:9, :]
    pick = (planes == partner).astype(F32).astype(BF16)
    coupling = {}
    for f in range(fields):
        for g in range(fields):
            if f != g:
                chosen = jnp.zeros_like(region)
                for number in range(table.shape[0]):
                    chosen = jnp.where(region == float(number), table[number, f * fields + g], chosen)
                coupling[f, g] = chosen
    for col in range(4):
        for t in range(4):
            rows = pl.ds(pl.multiple_of((place_of[1] ^ t) * block, block), block)
            cell = (early if col in (1, 2) else late)[t]
            here = [cell[col // 2, f] for f in range(fields)]
            moved = jnp.dot(jnp.concatenate(here, axis=0), pick, preferred_element_type=F32)
            centre = [cells_f.astype(F32) for cells_f in here]
            for f in range(fields):
                chunk = slice((col * fields + f) * LANES, (col * fields + f + 1) * LANES)
                modes[rows, chunk] = here[f]
                jump = speed_z[col : col + 1] * (moved[f * block : (f + 1) * block] - centre[f])
                z_image[rows, chunk] = jump.astype(BF16)
                running = None
                for g in range(fields):
                    if g != f:
                        term = coupling[f, g][col : col + 1] * centre[g]
                        running = term if running is None else running + term
                c_image[rows, chunk] = running.astype(BF16)
    for q, image in enumerate((z_image, c_image)):
        total = lax.dot_general(image[...], modes[...], CONTRACT_LAST, preferred_element_type=F32)
        place(place_of, keep, send, q, total, block)


def place(place_of, keep, send, q, total, block):
    for j in range(4):
        first = total[j * block : (j + 1) * block, :LANES]
        second = total[j * block : (j + 1) * block, LANES:]
        rows = slice(q * block, (q + 1) * block)
        keep[j, rows, :] = jnp.where(place_of[0] == 0, first, second)
        send[j, rows, :] = jnp.where(place_of[0] == 0, second, first).astype(BF16)


def edge_image(axis, speeds, modes, after, before, image, edge, side):
    fields, block = 4, modes.shape[0] // 4
    body = 4 * fields * block
    base = 4 * axis
    half_speeds = 0.5 * speeds[...]

    def beside_speed(message):
        rows = message[body:, :].astype(F32)
        return 0.5 * (rows[0:1] + rows[1:2] + rows[2:3])

    def col(line, end):
        return 2 * line + end if axis == 0 else 2 * end + line

    def lane_chunk(index):
        return slice(index * LANES, (index + 1) * LANES)

    for line, message in enumerate((before, after)):
        near_speed = half_speeds[base + col(line, 0) : base + col(line, 0) + 1]
        far_speed = half_speeds[base + col(line, 1) : base + col(line, 1) + 1]
        their_speed = beside_speed(message)
        for j in range(4):
            rows = slice(j * block, (j + 1) * block)
            for f in range(fields):
                near, far = (lane_chunk(col(line, end) * fields + f) for end in range(2))
                extra = lane_chunk(line * fields + f)
                m0 = modes[rows, near].astype(F32)
                m1 = modes[rows, far].astype(F32)
                start = (j * fields + f) * block
                beside = message[start : start + block, :]
                at_near = near_speed * m1
                at_far = -far_speed * m0
                if line == 1:
                    at_far = far_speed * beside.astype(F32) + at_far
                    at_side = -their_speed * m1
                else:
                    at_near = at_near - near_speed * beside.astype(F32)
                    at_side = their_speed * m0
                image[rows, near] = at_near.astype(BF16)
                image[rows, far] = at_far.astype(BF16)
                edge[rows, extra] = at_side.astype(BF16)
                side[rows, extra] = beside
    total = lax.dot_general(image[...], modes[...], CONTRACT_LAST, preferred_element_type=F32)
    return total + lax.dot_general(edge[...], side[...], CONTRACT_LAST, preferred_element_type=F32)


def x_kernel(place_of, speeds, modes, after, before, keep, send, image, edge, side):
    total = edge_image(0, speeds, modes, after, before, image, edge, side)
    place(place_of, keep, send, 0, total, modes.shape[0] // 4)


def y_kernel(place_of, speeds, modes, after, before, x_keep, x_send, zc_keep, zc_send, keep, send, image, edge, side):
    block = modes.shape[0] // 4
    total = edge_image(1, speeds, modes, after, before, image, edge, side)
    place(place_of, keep, send, 1, total, block)
    keep[:, :block, :] = x_keep[...]
    send[:, :block, :] = x_send[...]
    keep[:, 2 * block :, :] = zc_keep[...]
    send[:, 2 * block :, :] = zc_send[...]


def on_device(pod_modes, velocity, region, partner, coupling_table):
    block, fields, cells_x, cells_y, planes = pod_modes.shape
    names = ("gx", "y", "core", "ma")
    shape = tuple(lax.axis_size(name) for name in names)
    gx_count, y_count, core_count, ma_count = shape
    gx, y, core, ma = (lax.axis_index(name) for name in names)
    gy_count, gy = y_count * core_count, y * core_count + core
    cell_total = fields * cells_x * gx_count * cells_y * gy_count * planes
    scaling = 1.0 / math.sqrt(cell_total)
    kinds = block * ma_count
    reverse = (gx // (gx_count // 2) + gy) % 2 == 1
    k = jnp.where(reverse, ma_count - 1 - ma, ma)

    homes = jnp.stack([ma ^ t for t in range(ma_count)])
    wanted = jnp.where(reverse, ma_count - 1 - homes, homes).astype(jnp.int32)
    vmem = pl.BlockSpec(memory_space=pltpu.VMEM)
    smem = pl.BlockSpec(memory_space=pltpu.SMEM)
    params = pltpu.CompilerParams(vmem_limit_bytes=40 * 2**20)
    pieces = jnp.transpose(pod_modes, (3, 2, 1, 0, 4)).reshape(ma_count, 2, cells_x, fields, block, planes)
    piece = jax.ShapeDtypeStruct((2, fields, block, planes), BF16)
    packed = pl.pallas_call(
        pack_kernel,
        out_shape=(piece,) * (2 * ma_count),
        in_specs=[smem, vmem],
        out_specs=(vmem,) * (2 * ma_count),
        compiler_params=params,
        cost_estimate=pl.CostEstimate(flops=0, bytes_accessed=2 * 2**20, transcendentals=0),
    )(wanted, pieces)

    def collected(parts):
        blocks = {0: parts[0]}
        for t in (2, 3, 1):
            blocks[t] = lax.ppermute(parts[t], "ma", [(i, i ^ t) for i in range(ma_count)])
        return [blocks[t] for t in range(ma_count)]

    early, late = collected(packed[:ma_count]), collected(packed[ma_count:])

    def columns(part):
        return lax.dynamic_slice_in_dim(part, 2 * k, 2, 1).transpose(1, 0, 2).reshape(4, planes)

    vx, vy = columns(velocity[0]), columns(velocity[1])
    partners = jnp.broadcast_to(partner.astype(F32)[None], (8, planes))
    cells = jnp.concatenate([columns(velocity[2]), columns(region.astype(F32)), partners])

    speeds = jnp.concatenate([vx, vy])
    place_of = jnp.stack([core, ma]).astype(jnp.int32)
    width = 4 * fields * planes
    wide = pltpu.VMEM((kinds, width), BF16)
    narrow = pltpu.VMEM((kinds, width // 2), BF16)

    def sums(terms):
        rows = (ma_count, terms * block, LANES)
        return jax.ShapeDtypeStruct(rows, F32), jax.ShapeDtypeStruct(rows, BF16)

    rows = jax.ShapeDtypeStruct((4 * fields * block + 16, LANES), BF16)
    first, second = pl.pallas_call(
        message_kernel,
        out_shape=(rows, rows),
        in_specs=[smem] + [vmem] * 5,
        out_specs=(vmem, vmem),
        compiler_params=params,
        cost_estimate=pl.CostEstimate(flops=0, bytes_accessed=2**20, transcendentals=0),
    )(place_of, speeds, *early)

    zc_keep, zc_send, modes, y_first, y_second = pl.pallas_call(
        local_kernel,
        out_shape=(*sums(2), jax.ShapeDtypeStruct((kinds, width), BF16), rows, rows),
        in_specs=[smem, smem] + [vmem] * 10,
        out_specs=(vmem,) * 5,
        scratch_shapes=[wide, wide],
        compiler_params=params,
        cost_estimate=pl.CostEstimate(flops=2 * 2 * kinds * kinds * width, bytes_accessed=4 * 2**20, transcendentals=0),
    )(place_of, coupling_table.reshape(-1, fields * fields), cells, speeds, *early, *late)

    def along_x(part, step):
        return lax.ppermute(part, ("gx", "ma"), steps_along_x(shape, step))

    def along_y(part, step):
        return lax.ppermute(part, names, steps_along_y(shape, step))

    xr, xl = along_x(second, -1), along_x(first, 1)
    yr, yl = along_y(y_first, -1), along_y(y_second, 1)

    flops = 2 * kinds * kinds * width * 3 // 2
    cost = pl.CostEstimate(flops=flops, bytes_accessed=3 * 2**20, transcendentals=0)
    x_sums = pl.pallas_call(
        x_kernel,
        out_shape=sums(1),
        in_specs=[smem] + [vmem] * 4,
        out_specs=(vmem, vmem),
        scratch_shapes=[wide, narrow, narrow],
        compiler_params=params,
        cost_estimate=cost,
    )(place_of, speeds, modes, xr, xl)
    keep, send = pl.pallas_call(
        y_kernel,
        out_shape=sums(4),
        in_specs=[smem] + [vmem] * 8,
        out_specs=(vmem, vmem),
        scratch_shapes=[wide, narrow, narrow],
        compiler_params=params,
        cost_estimate=cost,
    )(place_of, speeds, modes, yr, yl, *x_sums, zc_keep, zc_send)

    def core_swap(part):
        return lax.ppermute(part, "core", [(i, 1 - i) for i in range(core_count)])

    shares = gx_count * y_count
    both = (keep + core_swap(send).astype(F32)).astype(BF16).reshape(ma_count * shares, -1, LANES)
    received = lax.all_to_all(both, ("ma", "gx", "y"), 0, 0)
    share = jnp.sum(received.astype(F32), axis=0) * scaling
    spread = jnp.broadcast_to(share.astype(BF16)[None], (shares * core_count,) + share.shape)
    whole = lax.all_to_all(spread, ("core", "gx", "y"), 0, 0)
    return whole.reshape(core_count, 4, block, LANES).transpose(1, 0, 3, 2).reshape(4, kinds, block).astype(F32)


def solution(mesh):
    gx, gy, ma = (mesh.shape[name] for name in ("gx", "gy", "ma"))
    split = Mesh(mesh.devices.reshape(gx, gy // 2, 2, ma), ("gx", "y", "core", "ma"))
    placed = (
        P("ma", None, "gx", ("y", "core"), None),
        P(None, "gx", ("y", "core"), None),
        P("gx", ("y", "core"), None),
        P(),
        P(),
    )
    return jax.shard_map(
        on_device, mesh=split, in_specs=placed, out_specs=P(None, None, "ma"), check_vma=False
    )
```

```python
import math

import jax
import jax.numpy as jnp
from jax import lax
from jax.experimental import pallas as pl
from jax.experimental.pallas import tpu as pltpu
from jax.sharding import Mesh, PartitionSpec as P

LANES = 128
BF16 = jnp.bfloat16
F32 = jnp.float32
CONTRACT_LAST = (((1,), (1,)), ((), ()))


def steps_along_x(shape, step):
    gx_count, y_count, core_count, ma_count = shape
    half = gx_count // 2
    pairs = []
    for gx in range(gx_count):
        to = gx + step
        if 0 <= to < gx_count:
            for ma in range(ma_count):
                to_ma = ma if gx // half == to // half else ma_count - 1 - ma
                pairs.append((gx * ma_count + ma, to * ma_count + to_ma))
    return pairs


def steps_along_y(shape, step):
    gx_count, y_count, core_count, ma_count = shape
    half = gx_count // 2
    gy_count = y_count * core_count

    def number(gx, place):
        gy, k = divmod(place, ma_count)
        ma = ma_count - 1 - k if (gx // half + gy) % 2 else k
        return (gx * gy_count + gy) * ma_count + ma

    places = gy_count * ma_count
    return [
        (number(gx, place), number(gx, place + step))
        for gx in range(gx_count)
        for place in range(places)
        if 0 <= place + step < places
    ]


def pack_early(wanted, pieces, early):
    for t in range(4):
        for number, (row, xi) in enumerate(((0, 1), (1, 0))):
            early[t, number] = pieces[wanted[4 + t], row, xi]


def pack_late(wanted, pieces, early, *late):
    for t in range(4):
        for number in range(2):
            late[t][number] = pieces[wanted[t], number, number]


def write_messages(axis, speeds, early, messages):
    fields, block = early.shape[2], early.shape[3]
    body = 4 * fields * block
    for number, message in enumerate(messages):
        for j in range(4):
            for f in range(fields):
                start = (j * fields + f) * block
                message[start : start + block, :] = early[j, number, f]
        rows = []
        rest = speeds[4 * axis + 1 + number : 4 * axis + 2 + number, :]
        for _ in range(3):
            rows.append(rest.astype(BF16).astype(F32))
            rest = rest - rows[-1]
        rows.append(jnp.zeros((13, LANES), F32))
        message[body:, :] = jnp.concatenate(rows).astype(BF16)


def message_kernel(speeds, early, *messages):
    write_messages(0, speeds, early, messages)


def local_kernel(place_of, table, cells, speeds, early, *refs):
    late, (keep, send, modes, first, second, z_image, c_image) = refs[:4], refs[4:]
    write_messages(1, speeds, early, (first, second))
    fields, block = early.shape[2], early.shape[3]
    planes = lax.broadcasted_iota(jnp.int32, (LANES, LANES), 0).astype(F32)
    speed_z, region, partner = cells[:4, :], cells[4:8, :], cells[8:9, :]
    pick = (planes == partner).astype(F32).astype(BF16)
    coupling = {}
    for f in range(fields):
        for g in range(fields):
            if f != g:
                chosen = jnp.zeros_like(region)
                for number in range(table.shape[0]):
                    chosen = jnp.where(region == float(number), table[number, f * fields + g], chosen)
                coupling[f, g] = chosen
    for col in range(4):
        for t in range(4):
            if col in (1, 2):
                rows = slice(t * block, (t + 1) * block)
                here = [early[t, col - 1, f] for f in range(fields)]
            else:
                rows = pl.ds(pl.multiple_of((place_of[1] ^ t) * block, block), block)
                here = [late[t][col // 2, f] for f in range(fields)]
            moved = jnp.dot(jnp.concatenate(here, axis=0), pick, preferred_element_type=F32)
            centre = [cells_f.astype(F32) for cells_f in here]
            for f in range(fields):
                chunk = slice((col * fields + f) * LANES, (col * fields + f + 1) * LANES)
                modes[rows, chunk] = here[f]
                jump = speed_z[col : col + 1] * (moved[f * block : (f + 1) * block] - centre[f])
                z_image[rows, chunk] = jump.astype(BF16)
                running = None
                for g in range(fields):
                    if g != f:
                        term = coupling[f, g][col : col + 1] * centre[g]
                        running = term if running is None else running + term
                c_image[rows, chunk] = running.astype(BF16)
    for q, image in enumerate((z_image, c_image)):
        total = lax.dot_general(image[...], modes[...], CONTRACT_LAST, preferred_element_type=F32)
        place(place_of, keep, send, q, total, block)


def place(place_of, keep, send, q, total, block):
    for j in range(4):
        first = total[j * block : (j + 1) * block, :LANES]
        second = total[j * block : (j + 1) * block, LANES:]
        rows = slice(q * block, (q + 1) * block)
        keep[j, rows, :] = jnp.where(place_of[0] == 0, first, second)
        send[j, rows, :] = jnp.where(place_of[0] == 0, second, first).astype(BF16)


def edge_image(axis, speeds, modes, after, before, image, edge, side):
    fields, block = 4, modes.shape[0] // 4
    body = 4 * fields * block
    base = 4 * axis
    half_speeds = 0.5 * speeds[...]

    def beside_speed(message):
        rows = message[body:, :].astype(F32)
        return 0.5 * (rows[0:1] + rows[1:2] + rows[2:3])

    def col(line, end):
        return 2 * line + end if axis == 0 else 2 * end + line

    def lane_chunk(index):
        return slice(index * LANES, (index + 1) * LANES)

    for line, message in enumerate((before, after)):
        near_speed = half_speeds[base + col(line, 0) : base + col(line, 0) + 1]
        far_speed = half_speeds[base + col(line, 1) : base + col(line, 1) + 1]
        their_speed = beside_speed(message)
        for j in range(4):
            rows = slice(j * block, (j + 1) * block)
            for f in range(fields):
                near, far = (lane_chunk(col(line, end) * fields + f) for end in range(2))
                extra = lane_chunk(line * fields + f)
                m0 = modes[rows, near].astype(F32)
                m1 = modes[rows, far].astype(F32)
                start = (j * fields + f) * block
                beside = message[start : start + block, :]
                at_near = near_speed * m1
                at_far = -far_speed * m0
                if line == 1:
                    at_far = far_speed * beside.astype(F32) + at_far
                    at_side = -their_speed * m1
                else:
                    at_near = at_near - near_speed * beside.astype(F32)
                    at_side = their_speed * m0
                image[rows, near] = at_near.astype(BF16)
                image[rows, far] = at_far.astype(BF16)
                edge[rows, extra] = at_side.astype(BF16)
                side[rows, extra] = beside
    total = lax.dot_general(image[...], modes[...], CONTRACT_LAST, preferred_element_type=F32)
    return total + lax.dot_general(edge[...], side[...], CONTRACT_LAST, preferred_element_type=F32)


def x_kernel(place_of, speeds, modes, after, before, keep, send, image, edge, side):
    total = edge_image(0, speeds, modes, after, before, image, edge, side)
    place(place_of, keep, send, 0, total, modes.shape[0] // 4)


def y_kernel(place_of, speeds, modes, after, before, x_keep, x_send, zc_keep, zc_send, keep, send, image, edge, side):
    block = modes.shape[0] // 4
    total = edge_image(1, speeds, modes, after, before, image, edge, side)
    place(place_of, keep, send, 1, total, block)
    keep[:, :block, :] = x_keep[...]
    send[:, :block, :] = x_send[...]
    keep[:, 2 * block :, :] = zc_keep[...]
    send[:, 2 * block :, :] = zc_send[...]


def on_device(pod_modes, velocity, region, partner, coupling_table):
    block, fields, cells_x, cells_y, planes = pod_modes.shape
    names = ("gx", "y", "core", "ma")
    shape = tuple(lax.axis_size(name) for name in names)
    gx_count, y_count, core_count, ma_count = shape
    gx, y, core, ma = (lax.axis_index(name) for name in names)
    gy_count, gy = y_count * core_count, y * core_count + core
    cell_total = fields * cells_x * gx_count * cells_y * gy_count * planes
    scaling = 1.0 / math.sqrt(cell_total)
    kinds = block * ma_count
    reverse = (gx // (gx_count // 2) + gy) % 2 == 1
    k = jnp.where(reverse, ma_count - 1 - ma, ma)

    homes = jnp.stack([ma ^ t for t in range(ma_count)] + [jnp.asarray(m, ma.dtype) for m in range(ma_count)])
    wanted = jnp.where(reverse, ma_count - 1 - homes, homes).astype(jnp.int32)
    vmem = pl.BlockSpec(memory_space=pltpu.VMEM)
    smem = pl.BlockSpec(memory_space=pltpu.SMEM)
    params = pltpu.CompilerParams(vmem_limit_bytes=40 * 2**20)
    pieces = jnp.transpose(pod_modes, (3, 2, 1, 0, 4)).reshape(ma_count, 2, cells_x, fields, block, planes)
    piece = (2, fields, block, planes)
    cost = pl.CostEstimate(flops=0, bytes_accessed=2**20, transcendentals=0)
    early = pl.pallas_call(
        pack_early,
        out_shape=jax.ShapeDtypeStruct((ma_count, *piece), BF16),
        in_specs=[smem, vmem],
        out_specs=vmem,
        compiler_params=params,
        cost_estimate=cost,
    )(wanted, pieces)
    late = pl.pallas_call(
        pack_late,
        out_shape=(jax.ShapeDtypeStruct(piece, BF16),) * ma_count,
        in_specs=[smem, vmem, pl.BlockSpec(memory_space=pl.ANY)],
        out_specs=(vmem,) * ma_count,
        compiler_params=params,
        cost_estimate=cost,
    )(wanted, pieces, early)
    late = list(late)
    early = lax.all_to_all(early, "ma", 0, 0)
    for t in (2, 3, 1):
        late[t] = lax.ppermute(late[t], "ma", [(i, i ^ t) for i in range(ma_count)])

    def columns(part):
        return lax.dynamic_slice_in_dim(part, 2 * k, 2, 1).transpose(1, 0, 2).reshape(4, planes)

    vx, vy = columns(velocity[0]), columns(velocity[1])
    partners = jnp.broadcast_to(partner.astype(F32)[None], (8, planes))
    cells = jnp.concatenate([columns(velocity[2]), columns(region.astype(F32)), partners])

    speeds = jnp.concatenate([vx, vy])
    place_of = jnp.stack([core, ma]).astype(jnp.int32)
    width = 4 * fields * planes
    wide = pltpu.VMEM((kinds, width), BF16)
    narrow = pltpu.VMEM((kinds, width // 2), BF16)

    def sums(terms):
        rows = (ma_count, terms * block, LANES)
        return jax.ShapeDtypeStruct(rows, F32), jax.ShapeDtypeStruct(rows, BF16)

    rows = jax.ShapeDtypeStruct((4 * fields * block + 16, LANES), BF16)
    first, second = pl.pallas_call(
        message_kernel,
        out_shape=(rows, rows),
        in_specs=[vmem] * 2,
        out_specs=(vmem, vmem),
        compiler_params=params,
        cost_estimate=pl.CostEstimate(flops=0, bytes_accessed=2**20, transcendentals=0),
    )(speeds, early)

    zc_keep, zc_send, modes, y_first, y_second = pl.pallas_call(
        local_kernel,
        out_shape=(*sums(2), jax.ShapeDtypeStruct((kinds, width), BF16), rows, rows),
        in_specs=[smem, smem] + [vmem] * 7,
        out_specs=(vmem,) * 5,
        scratch_shapes=[wide, wide],
        compiler_params=params,
        cost_estimate=pl.CostEstimate(flops=2 * 2 * kinds * kinds * width, bytes_accessed=4 * 2**20, transcendentals=0),
    )(place_of, coupling_table.reshape(-1, fields * fields), cells, speeds, early, *late)

    def along_x(part, step):
        return lax.ppermute(part, ("gx", "ma"), steps_along_x(shape, step))

    def along_y(part, step):
        return lax.ppermute(part, names, steps_along_y(shape, step))

    xr, xl = along_x(second, -1), along_x(first, 1)
    yr, yl = along_y(y_first, -1), along_y(y_second, 1)

    flops = 2 * kinds * kinds * width * 3 // 2
    cost = pl.CostEstimate(flops=flops, bytes_accessed=3 * 2**20, transcendentals=0)
    x_sums = pl.pallas_call(
        x_kernel,
        out_shape=sums(1),
        in_specs=[smem] + [vmem] * 4,
        out_specs=(vmem, vmem),
        scratch_shapes=[wide, narrow, narrow],
        compiler_params=params,
        cost_estimate=cost,
    )(place_of, speeds, modes, xr, xl)
    keep, send = pl.pallas_call(
        y_kernel,
        out_shape=sums(4),
        in_specs=[smem] + [vmem] * 8,
        out_specs=(vmem, vmem),
        scratch_shapes=[wide, narrow, narrow],
        compiler_params=params,
        cost_estimate=cost,
    )(place_of, speeds, modes, yr, yl, *x_sums, zc_keep, zc_send)

    def core_swap(part):
        return lax.ppermute(part, "core", [(i, 1 - i) for i in range(core_count)])

    shares = gx_count * y_count
    both = (keep + core_swap(send).astype(F32)).astype(BF16).reshape(ma_count * shares, -1, LANES)
    received = lax.all_to_all(both, ("ma", "gx", "y"), 0, 0)
    share = jnp.sum(received.astype(F32), axis=0) * scaling
    spread = jnp.broadcast_to(share.astype(BF16)[None], (shares * core_count,) + share.shape)
    whole = lax.all_to_all(spread, ("core", "gx", "y"), 0, 0)
    return whole.reshape(core_count, 4, block, LANES).transpose(1, 0, 3, 2).reshape(4, kinds, block).astype(F32)


def solution(mesh):
    gx, gy, ma = (mesh.shape[name] for name in ("gx", "gy", "ma"))
    split = Mesh(mesh.devices.reshape(gx, gy // 2, 2, ma), ("gx", "y", "core", "ma"))
    placed = (
        P("ma", None, "gx", ("y", "core"), None),
        P(None, "gx", ("y", "core"), None),
        P("gx", ("y", "core"), None),
        P(),
        P(),
    )
    return jax.shard_map(
        on_device, mesh=split, in_specs=placed, out_specs=P(None, None, "ma"), check_vma=False
    )
```

```python
import math

import jax
import jax.numpy as jnp
from jax import lax
from jax.experimental import pallas as pl
from jax.experimental.pallas import tpu as pltpu
from jax.sharding import Mesh, PartitionSpec as P

LANES = 128
BF16 = jnp.bfloat16
F32 = jnp.float32
CONTRACT_LAST = (((1,), (1,)), ((), ()))


def steps_along_x(shape, step):
    gx_count, y_count, core_count, ma_count = shape
    half = gx_count // 2
    pairs = []
    for gx in range(gx_count):
        to = gx + step
        if 0 <= to < gx_count:
            for ma in range(ma_count):
                to_ma = ma if gx // half == to // half else ma_count - 1 - ma
                pairs.append((gx * ma_count + ma, to * ma_count + to_ma))
    return pairs


def steps_along_y(shape, step):
    gx_count, y_count, core_count, ma_count = shape
    half = gx_count // 2
    gy_count = y_count * core_count

    def number(gx, place):
        gy, k = divmod(place, ma_count)
        ma = ma_count - 1 - k if (gx // half + gy) % 2 else k
        return (gx * gy_count + gy) * ma_count + ma

    places = gy_count * ma_count
    return [
        (number(gx, place), number(gx, place + step))
        for gx in range(gx_count)
        for place in range(places)
        if 0 <= place + step < places
    ]


def pack_early(wanted, pieces, early):
    for t in range(4):
        for number, (row, xi) in enumerate(((0, 1), (1, 0))):
            early[t, number] = pieces[wanted[4 + t], row, xi]


def pack_late(wanted, pieces, early, *late):
    for t in range(4):
        for number in range(2):
            late[t][number] = pieces[wanted[t], number, number]


def write_messages(axis, speeds, early, messages):
    fields, block = early.shape[2], early.shape[3]
    body = 4 * fields * block
    for number, message in enumerate(messages):
        for j in range(4):
            for f in range(fields):
                start = (j * fields + f) * block
                message[start : start + block, :] = early[j, number, f]
        rows = []
        rest = speeds[4 * axis + 1 + number : 4 * axis + 2 + number, :]
        for _ in range(3):
            rows.append(rest.astype(BF16).astype(F32))
            rest = rest - rows[-1]
        rows.append(jnp.zeros((13, LANES), F32))
        message[body:, :] = jnp.concatenate(rows).astype(BF16)


def message_kernel(speeds, early, *messages):
    write_messages(0, speeds, early, messages)


def local_kernel(place_of, table, cells, speeds, early, *refs):
    late, (keep, send, modes, first, second, z_image, c_image) = refs[:4], refs[4:]
    write_messages(1, speeds, early, (first, second))
    fields, block = early.shape[2], early.shape[3]
    planes = lax.broadcasted_iota(jnp.int32, (LANES, LANES), 0).astype(F32)
    speed_z, region, partner = cells[:4, :], cells[4:8, :], cells[8:9, :]
    pick = (planes == partner).astype(F32).astype(BF16)
    coupling = {}
    for f in range(fields):
        for g in range(fields):
            if f != g:
                chosen = jnp.zeros_like(region)
                for number in range(table.shape[0]):
                    chosen = jnp.where(region == float(number), table[number, f * fields + g], chosen)
                coupling[f, g] = chosen
    for col in range(4):
        for t in range(4):
            if col in (1, 2):
                rows = slice(t * block, (t + 1) * block)
                here = [early[t, col - 1, f] for f in range(fields)]
            else:
                rows = pl.ds(pl.multiple_of((place_of[1] ^ t) * block, block), block)
                here = [late[t][col // 2, f] for f in range(fields)]
            moved = jnp.dot(jnp.concatenate(here, axis=0), pick, preferred_element_type=F32)
            centre = [cells_f.astype(F32) for cells_f in here]
            for f in range(fields):
                chunk = slice((col * fields + f) * LANES, (col * fields + f + 1) * LANES)
                modes[rows, chunk] = here[f]
                jump = speed_z[col : col + 1] * (moved[f * block : (f + 1) * block] - centre[f])
                z_image[rows, chunk] = jump.astype(BF16)
                running = None
                for g in range(fields):
                    if g != f:
                        term = coupling[f, g][col : col + 1] * centre[g]
                        running = term if running is None else running + term
                c_image[rows, chunk] = running.astype(BF16)
    for q, image in enumerate((z_image, c_image)):
        total = lax.dot_general(image[...], modes[...], CONTRACT_LAST, preferred_element_type=F32)
        place(place_of, keep, send, q, total, block)


def place(place_of, keep, send, q, total, block):
    for j in range(4):
        first = total[j * block : (j + 1) * block, :LANES]
        second = total[j * block : (j + 1) * block, LANES:]
        rows = slice(q * block, (q + 1) * block)
        keep[j, rows, :] = jnp.where(place_of[0] == 0, first, second)
        send[j, rows, :] = jnp.where(place_of[0] == 0, second, first).astype(BF16)


def edge_image(axis, speeds, modes, after, before, image, edge, side):
    fields, block = 4, modes.shape[0] // 4
    body = 4 * fields * block
    base = 4 * axis
    half_speeds = 0.5 * speeds[...]

    def beside_speed(message):
        rows = message[body:, :].astype(F32)
        return 0.5 * (rows[0:1] + rows[1:2] + rows[2:3])

    def col(line, end):
        return 2 * line + end if axis == 0 else 2 * end + line

    def lane_chunk(index):
        return slice(index * LANES, (index + 1) * LANES)

    for line, message in enumerate((before, after)):
        near_speed = half_speeds[base + col(line, 0) : base + col(line, 0) + 1]
        far_speed = half_speeds[base + col(line, 1) : base + col(line, 1) + 1]
        their_speed = beside_speed(message)
        for j in range(4):
            rows = slice(j * block, (j + 1) * block)
            for f in range(fields):
                near, far = (lane_chunk(col(line, end) * fields + f) for end in range(2))
                extra = lane_chunk(line * fields + f)
                m0 = modes[rows, near].astype(F32)
                m1 = modes[rows, far].astype(F32)
                start = (j * fields + f) * block
                beside = message[start : start + block, :]
                at_near = near_speed * m1
                at_far = -far_speed * m0
                if line == 1:
                    at_far = far_speed * beside.astype(F32) + at_far
                    at_side = -their_speed * m1
                else:
                    at_near = at_near - near_speed * beside.astype(F32)
                    at_side = their_speed * m0
                image[rows, near] = at_near.astype(BF16)
                image[rows, far] = at_far.astype(BF16)
                edge[rows, extra] = at_side.astype(BF16)
                side[rows, extra] = beside
    total = lax.dot_general(image[...], modes[...], CONTRACT_LAST, preferred_element_type=F32)
    return total + lax.dot_general(edge[...], side[...], CONTRACT_LAST, preferred_element_type=F32)


def x_kernel(place_of, speeds, modes, after, before, keep, send, image, edge, side):
    total = edge_image(0, speeds, modes, after, before, image, edge, side)
    place(place_of, keep, send, 0, total, modes.shape[0] // 4)


def y_kernel(place_of, speeds, modes, after, before, x_keep, x_send, zc_keep, zc_send, keep, send, image, edge, side):
    block = modes.shape[0] // 4
    total = edge_image(1, speeds, modes, after, before, image, edge, side)
    place(place_of, keep, send, 1, total, block)
    keep[:, :block, :] = x_keep[...]
    send[:, :block, :] = x_send[...]
    keep[:, 2 * block :, :] = zc_keep[...]
    send[:, 2 * block :, :] = zc_send[...]


def order_kernel(whole, out):
    rows = whole.shape[1]
    for number in range(whole.shape[0]):
        start = number // 2 * rows
        out[number % 2, start : start + rows, :] = whole[number].astype(F32)


def on_device(pod_modes, velocity, region, partner, coupling_table):
    block, fields, cells_x, cells_y, planes = pod_modes.shape
    names = ("gx", "y", "core", "ma")
    shape = tuple(lax.axis_size(name) for name in names)
    gx_count, y_count, core_count, ma_count = shape
    gx, y, core, ma = (lax.axis_index(name) for name in names)
    gy_count, gy = y_count * core_count, y * core_count + core
    cell_total = fields * cells_x * gx_count * cells_y * gy_count * planes
    scaling = 1.0 / math.sqrt(cell_total)
    kinds = block * ma_count
    reverse = (gx // (gx_count // 2) + gy) % 2 == 1
    k = jnp.where(reverse, ma_count - 1 - ma, ma)

    homes = jnp.stack([ma ^ t for t in range(ma_count)] + [jnp.asarray(m, ma.dtype) for m in range(ma_count)])
    wanted = jnp.where(reverse, ma_count - 1 - homes, homes).astype(jnp.int32)
    vmem = pl.BlockSpec(memory_space=pltpu.VMEM)
    smem = pl.BlockSpec(memory_space=pltpu.SMEM)
    params = pltpu.CompilerParams(vmem_limit_bytes=40 * 2**20)
    pieces = jnp.transpose(pod_modes, (3, 2, 1, 0, 4)).reshape(ma_count, 2, cells_x, fields, block, planes)
    piece = (2, fields, block, planes)
    cost = pl.CostEstimate(flops=0, bytes_accessed=2**20, transcendentals=0)
    early = pl.pallas_call(
        pack_early,
        out_shape=jax.ShapeDtypeStruct((ma_count, *piece), BF16),
        in_specs=[smem, vmem],
        out_specs=vmem,
        compiler_params=params,
        cost_estimate=cost,
    )(wanted, pieces)
    late = pl.pallas_call(
        pack_late,
        out_shape=(jax.ShapeDtypeStruct(piece, BF16),) * ma_count,
        in_specs=[smem, vmem, pl.BlockSpec(memory_space=pl.ANY)],
        out_specs=(vmem,) * ma_count,
        compiler_params=params,
        cost_estimate=cost,
    )(wanted, pieces, early)
    late = list(late)
    early = lax.all_to_all(early, "ma", 0, 0)
    for t in (2, 3, 1):
        late[t] = lax.ppermute(late[t], "ma", [(i, i ^ t) for i in range(ma_count)])

    def columns(part):
        return lax.dynamic_slice_in_dim(part, 2 * k, 2, 1).transpose(1, 0, 2).reshape(4, planes)

    vx, vy = columns(velocity[0]), columns(velocity[1])
    partners = jnp.broadcast_to(partner.astype(F32)[None], (8, planes))
    cells = jnp.concatenate([columns(velocity[2]), columns(region.astype(F32)), partners])

    speeds = jnp.concatenate([vx, vy])
    place_of = jnp.stack([core, ma]).astype(jnp.int32)
    width = 4 * fields * planes
    wide = pltpu.VMEM((kinds, width), BF16)
    narrow = pltpu.VMEM((kinds, width // 2), BF16)

    def sums(terms):
        rows = (ma_count, terms * block, LANES)
        return jax.ShapeDtypeStruct(rows, F32), jax.ShapeDtypeStruct(rows, BF16)

    rows = jax.ShapeDtypeStruct((4 * fields * block + 16, LANES), BF16)
    first, second = pl.pallas_call(
        message_kernel,
        out_shape=(rows, rows),
        in_specs=[vmem] * 2,
        out_specs=(vmem, vmem),
        compiler_params=params,
        cost_estimate=pl.CostEstimate(flops=0, bytes_accessed=2**20, transcendentals=0),
    )(speeds, early)

    zc_keep, zc_send, modes, y_first, y_second = pl.pallas_call(
        local_kernel,
        out_shape=(*sums(2), jax.ShapeDtypeStruct((kinds, width), BF16), rows, rows),
        in_specs=[smem, smem] + [vmem] * 7,
        out_specs=(vmem,) * 5,
        scratch_shapes=[wide, wide],
        compiler_params=params,
        cost_estimate=pl.CostEstimate(flops=2 * 2 * kinds * kinds * width, bytes_accessed=4 * 2**20, transcendentals=0),
    )(place_of, coupling_table.reshape(-1, fields * fields), cells, speeds, early, *late)

    def along_x(part, step):
        return lax.ppermute(part, ("gx", "ma"), steps_along_x(shape, step))

    def along_y(part, step):
        return lax.ppermute(part, names, steps_along_y(shape, step))

    xr, xl = along_x(second, -1), along_x(first, 1)
    yr, yl = along_y(y_first, -1), along_y(y_second, 1)

    flops = 2 * kinds * kinds * width * 3 // 2
    cost = pl.CostEstimate(flops=flops, bytes_accessed=3 * 2**20, transcendentals=0)
    x_sums = pl.pallas_call(
        x_kernel,
        out_shape=sums(1),
        in_specs=[smem] + [vmem] * 4,
        out_specs=(vmem, vmem),
        scratch_shapes=[wide, narrow, narrow],
        compiler_params=params,
        cost_estimate=cost,
    )(place_of, speeds, modes, xr, xl)
    keep, send = pl.pallas_call(
        y_kernel,
        out_shape=sums(4),
        in_specs=[smem] + [vmem] * 8,
        out_specs=(vmem, vmem),
        scratch_shapes=[wide, narrow, narrow],
        compiler_params=params,
        cost_estimate=cost,
    )(place_of, speeds, modes, yr, yl, *x_sums, zc_keep, zc_send)

    def core_swap(part):
        return lax.ppermute(part, "core", [(i, 1 - i) for i in range(core_count)])

    shares = gx_count * y_count
    both = (keep + core_swap(send).astype(F32)).astype(BF16).reshape(ma_count * shares, -1, LANES)
    received = lax.all_to_all(both, ("ma", "gx", "y"), 0, 0)
    share = jnp.sum(received.astype(F32), axis=0) * scaling
    spread = jnp.broadcast_to(share.astype(BF16)[None], (shares * core_count,) + share.shape)
    whole = lax.all_to_all(spread, ("gx", "y", "core"), 0, 0)
    whole = pl.pallas_call(
        order_kernel,
        out_shape=jax.ShapeDtypeStruct((core_count, 4 * block, LANES), F32),
        in_specs=[vmem],
        out_specs=vmem,
        compiler_params=params,
    )(whole)
    return whole.reshape(core_count, 4, block, LANES).transpose(1, 0, 3, 2).reshape(4, kinds, block)


def solution(mesh):
    gx, gy, ma = (mesh.shape[name] for name in ("gx", "gy", "ma"))
    split = Mesh(mesh.devices.reshape(gx, gy // 2, 2, ma), ("gx", "y", "core", "ma"))
    placed = (
        P("ma", None, "gx", ("y", "core"), None),
        P(None, "gx", ("y", "core"), None),
        P("gx", ("y", "core"), None),
        P(),
        P(),
    )
    return jax.shard_map(
        on_device, mesh=split, in_specs=placed, out_specs=P(None, None, "ma"), check_vma=False
    )
```
